512 devices in a mesh: dp: 8 (over z_hi, core), lat: 64 (over x, z_lo, y).
Axes of the slice: x: 4, y: 8, z: 8 (z_hi: 4, z_lo: 2; z = z_hi * 2 + z_lo), core: 2. Of those that a mesh axis runs over, the one named last changes fastest.
Arguments:
- query_feats: bfloat16 [8, 128, 128, 1024], P('dp', 'lat'), may hold values from -32 to 32
- key_feats: bfloat16 [8, 128, 128, 1024], P('dp', 'lat'), may hold values from -6 to 6
- value_feats: bfloat16 [8, 128, 128, 1024], P('dp', 'lat'), may hold values from -6 to 6
- out_grad: bfloat16 [8, 128, 128, 1024], P('dp', 'lat'), may hold values from -6 to 6
- out_proj: bfloat16 [1024, 1024], P('lat'), may hold values from -0.1875 to 0.1875
- cycle_lo: int32 [128], replicated, may hold values from 0 to 125, as said below
- cycle_hi: int32 [128], replicated, may hold values from 2 to 127, as said below
- lon_half: int32 [128], replicated, may hold values from 1 to 64, as said below
Outputs:
- query_grad: bfloat16 [8, 128, 128, 1024], P('dp', 'lat')
- key_grad: bfloat16 [8, 128, 128, 1024], P('dp', 'lat')
- value_grad: bfloat16 [8, 128, 128, 1024], P('dp', 'lat')
- proj_grad: float32 [1024, 1024], P('lat')
The draws below stay inside these ranges and needn't reach their ends.
Inputs may be any that keep to these rules, and one draw needn't show every extreme that they name: cycle_lo[i] is i minus 1 to 2, not below 0; within 4 cycles of either pole it is max(i - 2, 0). cycle_hi[i] is i plus 1 to 2, not above 127; within 4 cycles of either pole it is min(i + 2, 127). `lon_half`: 64, the whole cycle, within 4 cycles of either pole; at most 32 elsewhere.
All inputs are finite; a program needn't handle non-finite values.
Results may differ from the reference program's by a relative error of at most 0.015.
Values may be sent and summed in bfloat16 or wider, within the bound.
No kernel may reach another device: no remote copies, remote signals or barrier semaphores. Data moves between devices by JAX's collectives and lax.ppermute only.
A program may use at most 192 MiB of HBM per device.

```python
import math
import jax
import jax.numpy as jnp
from jax import lax

D = 1024
HEADS = 16
HEAD_DIM = 64
REACH = 2
LON = 128
NLAT = 128
POLAR = 4
SAMPLES = 8


def draw_pair(key):
    base = jax.random.fold_in(key, 11)
    key_one, key_two = jax.random.split(base, 2)
    shape = (SAMPLES, NLAT, LON, D)
    queries = jnp.clip(jax.random.normal(key_one, shape, jnp.float32), -6.0, 6.0)
    keyset = jnp.clip(jax.random.normal(key_two, shape, jnp.float32), -6.0, 6.0)
    return (queries, keyset)


def draw_query_feats(key, part):
    return draw_pair(key)[0].astype(jnp.bfloat16)


def draw_key_feats(key, part):
    return draw_pair(key)[1].astype(jnp.bfloat16)


def polar_cycles():
    cycles = jnp.arange(NLAT, dtype=jnp.int32)
    polar = (cycles < POLAR) | (cycles >= NLAT - POLAR)
    return (cycles, polar)


def draw_cycle_lo(key, part):
    cycles, polar = polar_cycles()
    reach = jnp.where(polar, REACH, jax.random.randint(jax.random.fold_in(key, 21), (NLAT,), 1, REACH + 1))
    return jnp.maximum(cycles - reach, 0).astype(jnp.int32)


def draw_cycle_hi(key, part):
    cycles, polar = polar_cycles()
    reach = jnp.where(polar, REACH, jax.random.randint(jax.random.fold_in(key, 22), (NLAT,), 1, REACH + 1))
    return jnp.minimum(cycles + reach, NLAT - 1).astype(jnp.int32)


def draw_lon_half(key, part):
    cycles, polar = polar_cycles()
    narrow = jax.random.randint(jax.random.fold_in(key, 23), (NLAT,), 1, LON // 4 + 1)
    return jnp.where(polar, LON // 2, narrow).astype(jnp.int32)


def block_levels(stream_key, extent, cuts, least, largest):
    def one(position, blocks):
        draws = jax.random.uniform(jax.random.fold_in(jax.random.fold_in(stream_key, 6), position), (blocks,), jnp.float32, least / len(cuts), largest / len(cuts))
        return jnp.repeat(jnp.exp(draws), extent[position] // blocks).reshape((-1,) + (1,) * (len(extent) - position - 1))

    level = one(*cuts[0])
    for cut in cuts[1:]:
        level = level * one(*cut)
    return level


def normal_values(own_key, shape, spread, limit, pieces=(), kind=jnp.bfloat16):
    gain = block_levels(own_key, shape, pieces, -0.22, 0.18) if pieces else 1.0
    drawn = jax.random.normal(own_key, shape, jnp.float32) * spread * gain
    return jnp.minimum(jnp.maximum(drawn, -limit), limit).astype(kind)


def setup_inputs(seed: int = 0) -> dict:
    keys = jax.random.split(jax.random.key(seed), 9)
    return {
        "query_feats": draw_query_feats(jax.random.fold_in(keys[8], 71), 0),
        "key_feats": draw_key_feats(jax.random.fold_in(keys[8], 71), 0),
        "value_feats": normal_values(keys[2], (SAMPLES, NLAT, LON, D), 1.0, 6.0, ((0, 8), (1, 64))),
        "out_grad": normal_values(keys[3], (SAMPLES, NLAT, LON, D), 1.0, 6.0, ((0, 8), (1, 64))),
        "out_proj": normal_values(keys[4], (D, D), D ** -0.5, 0.1875, ((0, 64),)),
        "cycle_lo": draw_cycle_lo(jax.random.fold_in(keys[8], 71), 0),
        "cycle_hi": draw_cycle_hi(jax.random.fold_in(keys[8], 71), 0),
        "lon_half": draw_lon_half(jax.random.fold_in(keys[8], 71), 0),
    }


def cycle_log_weight(cycles, total):
    latitude = (cycles.astype(jnp.float32) + 0.5) * (math.pi / total)
    return jnp.log(jnp.sin(latitude))

def attend(query_heads, key_heads, value_heads, grad_heads, allowed, log_weight):
    scaling = 1.0 / math.sqrt(HEAD_DIM)
    query_wide = query_heads.astype(jnp.float32)
    key_wide = key_heads.astype(jnp.float32)
    value_wide = value_heads.astype(jnp.float32)
    grad_wide = grad_heads.astype(jnp.float32)
    scores = jnp.einsum('qhd,khd->hqk', query_wide, key_wide) * scaling + log_weight[None, None, :]
    scores = jnp.where(allowed[None], scores, -jnp.inf)
    row_peak = lax.optimization_barrier(jnp.max(scores, axis=-1, keepdims=True))
    unnormed = jnp.exp(scores - row_peak)
    attention = unnormed / lax.optimization_barrier(jnp.sum(unnormed, axis=-1, keepdims=True))
    attention_low = attention.astype(jnp.bfloat16)
    low_wide = attention_low.astype(jnp.float32)
    attended = jnp.einsum('hqk,khd->qhd', low_wide, value_wide).astype(jnp.bfloat16)
    row_dot = lax.optimization_barrier(jnp.sum(grad_wide * attended.astype(jnp.float32), axis=-1))
    prob_grad = jnp.einsum('qhd,khd->hqk', grad_wide, value_wide)
    score_grad = (attention * (prob_grad - row_dot.T[:, :, None]) * scaling).astype(jnp.bfloat16)
    score_wide = score_grad.astype(jnp.float32)
    query_part = jnp.einsum('hqk,khd->qhd', score_wide, key_wide)
    key_part = jnp.einsum('hqk,qhd->khd', score_wide, query_wide)
    value_part = jnp.einsum('hqk,qhd->khd', low_wide, grad_wide)
    return (attended, query_part, key_part, value_part)

def reference(query_feats, key_feats, value_feats, out_grad, out_proj, cycle_lo, cycle_hi, lon_half):
    attn_grad = jnp.dot(out_grad.reshape(-1, D), out_proj.T, preferred_element_type=jnp.float32)
    attn_grad = attn_grad.astype(jnp.bfloat16).reshape(out_grad.shape)
    longitude = jnp.arange(LON, dtype=jnp.int32)
    lon_gap = jnp.abs(longitude[:, None] - longitude[None, :])
    lon_dist = jnp.minimum(lon_gap, LON - lon_gap)
    span = 2 * REACH + 1

    def one_sample(inputs):
        queries, keyset, valueset, grads = inputs
        padding = ((REACH, REACH), (0, 0), (0, 0))
        keys_pad = jnp.pad(keyset, padding)
        values_pad = jnp.pad(valueset, padding)

        def one_cycle(carry, cycle_index):
            key_acc, value_acc = carry
            corner = (cycle_index, jnp.int32(0), jnp.int32(0))
            key_block = lax.dynamic_slice(keys_pad, corner, (span, LON, D)).reshape(span * LON, HEADS, HEAD_DIM)
            value_block = lax.dynamic_slice(values_pad, corner, (span, LON, D)).reshape(span * LON, HEADS, HEAD_DIM)
            query_block = lax.dynamic_index_in_dim(queries, cycle_index, 0, keepdims=False).reshape(LON, HEADS, HEAD_DIM)
            grad_block = lax.dynamic_index_in_dim(grads, cycle_index, 0, keepdims=False).reshape(LON, HEADS, HEAD_DIM)
            cycle_ids = cycle_index - REACH + jnp.arange(span, dtype=jnp.int32)
            lower = lax.dynamic_index_in_dim(cycle_lo, cycle_index, 0, keepdims=False)
            upper = lax.dynamic_index_in_dim(cycle_hi, cycle_index, 0, keepdims=False)
            half = lax.dynamic_index_in_dim(lon_half, cycle_index, 0, keepdims=False)
            cycle_ok = (cycle_ids >= lower) & (cycle_ids <= upper)
            lon_ok = lon_dist <= half
            allowed = (lon_ok[:, None, :] & cycle_ok[None, :, None]).reshape(LON, span * LON)
            cycle_weight = cycle_log_weight(jnp.clip(cycle_ids, 0, NLAT - 1), NLAT)
            log_weight = jnp.broadcast_to(cycle_weight[:, None], (span, LON)).reshape(span * LON)
            attended, query_part, key_part, value_part = attend(query_block, key_block, value_block, grad_block, allowed, log_weight)
            key_old = lax.dynamic_slice(key_acc, corner, (span, LON, D))
            key_acc = lax.dynamic_update_slice(key_acc, key_old + key_part.reshape(span, LON, D), corner)
            value_old = lax.dynamic_slice(value_acc, corner, (span, LON, D))
            value_acc = lax.dynamic_update_slice(value_acc, value_old + value_part.reshape(span, LON, D), corner)
            return ((key_acc, value_acc), (attended.reshape(LON, D), query_part.reshape(LON, D).astype(jnp.bfloat16)))
        zeros = jnp.zeros((NLAT + 2 * REACH, LON, D), jnp.float32)
        carry, outputs = lax.scan(one_cycle, (zeros, zeros), jnp.arange(NLAT, dtype=jnp.int32))
        key_acc, value_acc = carry
        attended, query_out = outputs
        key_out = key_acc[REACH:REACH + NLAT].astype(jnp.bfloat16)
        value_out = value_acc[REACH:REACH + NLAT].astype(jnp.bfloat16)
        return (attended, query_out, key_out, value_out)
    attended, query_grad, key_grad, value_grad = lax.map(one_sample, (query_feats, key_feats, value_feats, attn_grad))
    scaling = 1.0 / math.sqrt(SAMPLES * NLAT * LON)
    summed = jnp.dot(attended.reshape(-1, D).T, out_grad.reshape(-1, D), preferred_element_type=jnp.float32)
    proj_grad = summed * scaling
    return (query_grad, key_grad, value_grad, proj_grad)
```

```python
import functools
import math

import jax
import jax.numpy as jnp
import numpy as np
from jax import lax
from jax.experimental import pallas as pl
from jax.experimental.pallas import tpu as pltpu
from jax.sharding import Mesh
from jax.sharding import PartitionSpec as P

HEADS = 16
HEAD_DIM = 64
REACH = 2
PAIR = 2 * HEAD_DIM
SCALE = 1.0 / math.sqrt(HEAD_DIM)
SPAN = 2 * REACH + 1
DP = ("zh", "core")
XZ = ("x", "zl")
LAT = ("x", "zl", "y")
BF = jnp.bfloat16
F32 = jnp.float32
VMEM_LIMIT = 48 * 1024 * 1024


def dot(a, b, dims):
    return lax.dot_general(a, b, (dims, ((), ())), preferred_element_type=F32)


def fill_bias(first, lo_ref, hi_ref, half_ref, logw_ref, bias_ref):
    cycles, _, lon = bias_ref.shape
    total = lo_ref.shape[0]
    key_lon = lax.broadcasted_iota(jnp.int32, (lon, lon), 0)
    query_lon = lax.broadcasted_iota(jnp.int32, (lon, lon), 1)
    gap = jnp.abs(key_lon - query_lon)
    dist = jnp.minimum(gap, lon - gap)
    for i in range(cycles):
        cycle = first + i
        lon_ok = dist <= half_ref[cycle]
        for c in range(SPAN):
            key_cycle = cycle - REACH + c
            ok = (key_cycle >= lo_ref[cycle]) & (key_cycle <= hi_ref[cycle])
            weight = logw_ref[jnp.clip(key_cycle, 0, total - 1)]
            value = jnp.where(ok, weight, -jnp.inf)
            bias_ref[i, c * lon : (c + 1) * lon, :] = jnp.where(lon_ok, value, -jnp.inf)


def head_masks(scale):
    lane = lax.broadcasted_iota(jnp.int32, (1, PAIR), 1)
    first = jnp.where(lane < HEAD_DIM, scale, 0.0).astype(F32)
    return first, scale - first


def both_heads(rows, scale):
    first, second = head_masks(scale)
    wide = rows.astype(F32)
    return jnp.concatenate([(wide * first).astype(BF), (wide * second).astype(BF)], axis=0)


def own_columns(both, lon):
    return jnp.concatenate([both[:HEAD_DIM, :lon], both[HEAD_DIM:, lon:]], axis=0).T


def forward_kernel(
    first_ref, lo_ref, hi_ref, half_ref, logw_ref,
    q_ref, kp_ref, ko_ref, kn_ref, vp_ref, vo_ref, vn_ref,
    out_ref, prob_ref, bias_ref,
):
    cycles, _, lon = bias_ref.shape

    @pl.when(pl.program_id(0) == 0)
    def _():
        fill_bias(first_ref[0], lo_ref, hi_ref, half_ref, logw_ref, bias_ref)

    keys = jnp.concatenate([kp_ref[0], ko_ref[...], kn_ref[0]], axis=0)
    values = jnp.concatenate([vp_ref[0], vo_ref[...], vn_ref[0]], axis=0)
    for i in range(cycles):
        window = slice(i * lon, (i + SPAN) * lon)
        rows = slice(i * lon, (i + 1) * lon)
        queries = both_heads(q_ref[rows, :], SCALE)
        scores = dot(keys[window], queries, ((1,), (1,)))
        bias = bias_ref[i]
        scores = scores + jnp.concatenate([bias, bias], axis=1)
        weights = jnp.exp(scores - jnp.max(scores, axis=0, keepdims=True))
        inverse = 1.0 / jnp.sum(weights, axis=0, keepdims=True)
        probs = (weights * inverse).astype(BF)
        prob_ref[0, i] = probs
        attended = dot(values[window], probs, ((0,), (0,)))
        out_ref[rows, :] = own_columns(attended, lon).astype(BF)


def backward_kernel(
    q_ref, g_ref, o_ref, prob_ref, kp_ref, ko_ref, kn_ref, vp_ref, vo_ref, vn_ref,
    dq_ref, low_ref, own_ref, high_ref,
):
    cycles = prob_ref.shape[1]
    lon = prob_ref.shape[2] // SPAN
    keys = jnp.concatenate([kp_ref[0], ko_ref[...], kn_ref[0]], axis=0)
    values = jnp.concatenate([vp_ref[0], vo_ref[...], vn_ref[0]], axis=0)
    parts = []
    for i in range(cycles):
        window = slice(i * lon, (i + SPAN) * lon)
        rows = slice(i * lon, (i + 1) * lon)
        queries = both_heads(q_ref[rows, :], SCALE)
        grads = both_heads(g_ref[rows, :], 1.0)
        product = (g_ref[rows, :].astype(F32) * o_ref[rows, :].astype(F32)).T
        row_dot = jnp.concatenate(
            [
                jnp.sum(product[:HEAD_DIM], axis=0, keepdims=True),
                jnp.sum(product[HEAD_DIM:], axis=0, keepdims=True),
            ],
            axis=1,
        )
        probs = prob_ref[0, i]
        prob_grad = dot(values[window], grads, ((1,), (1,)))
        score_grad = (probs.astype(F32) * (prob_grad - row_dot)).astype(BF)
        query_part = dot(keys[window], score_grad, ((0,), (0,)))
        dq_ref[rows, :] = (own_columns(query_part, lon) * SCALE).astype(BF)
        key_part = dot(score_grad, queries, ((1,), (0,)))
        value_part = dot(probs, grads, ((1,), (0,)))
        parts.append((key_part, value_part))
    for which in range(2):
        near, far = parts[0][which], parts[1][which]
        low_ref[which, :lon] = near[:lon].astype(BF)
        low_ref[which, lon:] = (near[lon : 2 * lon] + far[:lon]).astype(BF)
        own_ref[which] = (near[2 * lon : 4 * lon] + far[lon : 3 * lon]).astype(own_ref.dtype)
        high_ref[which, :lon] = (near[4 * lon :] + far[3 * lon : 4 * lon]).astype(BF)
        high_ref[which, lon:] = far[4 * lon :].astype(BF)


def forward(first, lo, hi, half, logw, q, k, v, below, above, lon):
    rows, width = q.shape
    cycles = rows // lon
    pairs = width // PAIR
    smem = pl.BlockSpec(memory_space=pltpu.SMEM)
    flat = pl.BlockSpec((rows, PAIR), lambda p: (0, p))
    key = pl.BlockSpec((1, rows, PAIR), lambda p: (0, 0, p))
    value = pl.BlockSpec((1, rows, PAIR), lambda p: (1, 0, p))
    return pl.pallas_call(
        forward_kernel,
        grid=(pairs,),
        in_specs=[smem] * 5 + [flat, key, flat, key, value, flat, value],
        out_specs=[flat, pl.BlockSpec((1, cycles, SPAN * lon, 2 * lon), lambda p: (p, 0, 0, 0))],
        out_shape=[
            jax.ShapeDtypeStruct((rows, width), BF),
            jax.ShapeDtypeStruct((pairs, cycles, SPAN * lon, 2 * lon), BF),
        ],
        scratch_shapes=[pltpu.VMEM((cycles, SPAN * lon, lon), F32)],
        compiler_params=pltpu.CompilerParams(vmem_limit_bytes=VMEM_LIMIT),
        cost_estimate=pl.CostEstimate(flops=4 * 10**9, bytes_accessed=12 * 10**6, transcendentals=3 * 10**6),
        name="attention_forward",
    )(first, lo, hi, half, logw, q, below, k, above, below, v, above)


def backward(q, g, o, probs, k, v, below, above, lon):
    rows, width = q.shape
    cycles = rows // lon
    pairs = width // PAIR
    flat = pl.BlockSpec((rows, PAIR), lambda p: (0, p))
    key = pl.BlockSpec((1, rows, PAIR), lambda p: (0, 0, p))
    value = pl.BlockSpec((1, rows, PAIR), lambda p: (1, 0, p))
    both = pl.BlockSpec((2, rows, PAIR), lambda p: (0, 0, p))
    prob = pl.BlockSpec((1, cycles, SPAN * lon, 2 * lon), lambda p: (p, 0, 0, 0))
    stacked = jax.ShapeDtypeStruct((2, rows, width), BF)
    return pl.pallas_call(
        backward_kernel,
        grid=(pairs,),
        in_specs=[flat, flat, flat, prob, key, flat, key, value, flat, value],
        out_specs=[flat, both, both, both],
        out_shape=[
            jax.ShapeDtypeStruct((rows, width), BF),
            stacked,
            jax.ShapeDtypeStruct((2, rows, width), F32),
            stacked,
        ],
        compiler_params=pltpu.CompilerParams(vmem_limit_bytes=VMEM_LIMIT),
        cost_estimate=pl.CostEstimate(flops=8 * 10**9, bytes_accessed=16 * 10**6, transcendentals=0),
        name="attention_backward",
    )(q, g, o, probs, below, k, above, below, v, above)


def lat_shift(value, by):
    size = lax.axis_size(LAT)
    pairs = [(i, i + by) for i in range(size) if 0 <= i + by < size]
    return lax.ppermute(value, LAT, pairs)


def core_swap(value):
    return lax.ppermute(value, "core", [(0, 1), (1, 0)])


def spread(value, axes):
    size = lax.axis_size(axes)
    return lax.all_to_all(
        jnp.broadcast_to(value[None], (size,) + value.shape), axes, 0, 0, tiled=True
    )


def scatter_sum(value, axes):
    size = lax.axis_size(axes)
    blocks = value.reshape((size, value.shape[0] // size) + value.shape[1:])
    received = lax.all_to_all(blocks, axes, 0, 0, tiled=True)
    return jnp.sum(received.astype(F32), axis=0)


def local(query_feats, key_feats, value_feats, out_grad, out_proj, cycle_lo, cycle_hi, lon_half):
    cycles, lon, width = query_feats.shape[1:]
    rows = cycles * lon
    total = cycle_lo.shape[0]
    half_width = width // 2
    q = query_feats.reshape(rows, width)
    k = key_feats.reshape(rows, width)
    v = value_feats.reshape(rows, width)
    grad_flat = out_grad.reshape(rows, width)
    core = lax.axis_index("core")
    mine, others = core * half_width, (1 - core) * half_width

    stacked = jnp.stack([k, v])
    below = lat_shift(stacked, 1)
    above = lat_shift(stacked, -1)

    proj = lax.dynamic_slice_in_dim(out_proj, mine, half_width, axis=1)
    proj = spread(proj, "y").reshape(-1, half_width)
    proj = spread(proj, XZ).reshape(-1, half_width)
    proj_other = core_swap(proj)
    grad_mine = lax.dynamic_slice_in_dim(grad_flat, mine, half_width, axis=1)
    grad_other = lax.dynamic_slice_in_dim(grad_flat, others, half_width, axis=1)

    latitude = (np.arange(total, dtype=np.float32) + np.float32(0.5)) * np.float32(math.pi / total)
    logw = jnp.asarray(np.log(np.sin(latitude)).astype(np.float32))
    first = (lax.axis_index(LAT) * cycles).astype(jnp.int32).reshape(1)
    attended, probs = forward(
        first, cycle_lo, cycle_hi, lon_half, logw, q, k, v, below, above, lon
    )

    sent = dot(attended, grad_other, ((0,), (0,))).astype(BF)
    received = core_swap(sent)

    attn_grad = dot(grad_mine, proj, ((1,), (1,))) + dot(grad_other, proj_other, ((1,), (1,)))
    attn_grad = attn_grad.astype(BF)
    query_grad, low, own, high = backward(q, attn_grad, attended, probs, k, v, below, above, lon)
    from_below = lat_shift(high, 1)
    from_above = lat_shift(low, -1)

    partial = (dot(attended, grad_mine, ((0,), (0,))) + received.astype(F32)).astype(BF)
    partial = scatter_sum(partial, XZ).astype(BF)
    partial = scatter_sum(partial, "y").astype(BF)
    samples = lax.axis_size(DP)
    gathered = spread(partial, DP).reshape((samples // 2, 2) + partial.shape)
    summed = jnp.sum(gathered.astype(F32), axis=0)
    scaling = 1.0 / math.sqrt(samples * total * lon)
    proj_grad = jnp.concatenate([summed[0], summed[1]], axis=1) * scaling

    own = own + from_below.astype(F32) + from_above.astype(F32)
    shape = query_feats.shape
    return (
        query_grad.reshape(shape),
        own[0].astype(BF).reshape(shape),
        own[1].astype(BF).reshape(shape),
        proj_grad,
    )


def solution(mesh):
    parts = Mesh(mesh.devices.reshape(4, 2, 4, 2, 8), DP + LAT)
    placed = P(DP, LAT, None, None)
    return jax.shard_map(
        local,
        mesh=parts,
        in_specs=(placed, placed, placed, placed, P(LAT, None), P(), P(), P()),
        out_specs=(placed, placed, placed, P(LAT, None)),
        check_vma=False,
    )
```

```python
import functools
import math

import jax
import jax.numpy as jnp
import numpy as np
from jax import lax
from jax.experimental import pallas as pl
from jax.experimental.pallas import tpu as pltpu
from jax.sharding import Mesh
from jax.sharding import PartitionSpec as P

HEADS = 16
HEAD_DIM = 64
REACH = 2
PAIR = 2 * HEAD_DIM
PPS = 2
HALVES = 2
SCALE = 1.0 / math.sqrt(HEAD_DIM)
SPAN = 2 * REACH + 1
DP = ("zh", "core")
XZ = ("x", "zl")
LAT = ("x", "zl", "y")
BF = jnp.bfloat16
F32 = jnp.float32
VMEM_LIMIT = 60 * 1024 * 1024
LARGE = pl.CostEstimate(flops=2*10**10, bytes_accessed=4*10**7, transcendentals=0)
SMALL = pl.CostEstimate(flops=10**6, bytes_accessed=10**5, transcendentals=0)


def dot(a, b, dims):
    return lax.dot_general(a, b, (dims, ((), ())), preferred_element_type=F32)


def fill_bias(first, lo_ref, hi_ref, half_ref, logw_ref, bias_ref):
    cycles, _, lon = bias_ref.shape
    total = lo_ref.shape[0]
    key_lon = lax.broadcasted_iota(jnp.int32, (lon, lon), 0)
    query_lon = lax.broadcasted_iota(jnp.int32, (lon, lon), 1)
    gap = jnp.abs(key_lon - query_lon)
    dist = jnp.minimum(gap, lon - gap)
    for i in range(cycles):
        cycle = first + i
        lon_ok = dist <= half_ref[cycle]
        for c in range(SPAN):
            key_cycle = cycle - REACH + c
            ok = (key_cycle >= lo_ref[cycle]) & (key_cycle <= hi_ref[cycle])
            weight = logw_ref[jnp.clip(key_cycle, 0, total - 1)]
            value = jnp.where(ok, weight, -jnp.inf)
            bias_ref[i, c * lon : (c + 1) * lon, :] = jnp.where(lon_ok, value, -jnp.inf)


def head_masks(scale):
    lane = lax.broadcasted_iota(jnp.int32, (1, PAIR), 1)
    first = jnp.where(lane < HEAD_DIM, scale, 0.0).astype(F32)
    return first, scale - first


def both_heads(rows, scale):
    first, second = head_masks(scale)
    wide = rows.astype(F32)
    return jnp.concatenate([(wide * first).astype(BF), (wide * second).astype(BF)], axis=0)


def own_columns(both, lon):
    return jnp.concatenate([both[:HEAD_DIM, :lon], both[HEAD_DIM:, lon:]], axis=0).T


def forward_kernel(
    first_ref, lo_ref, hi_ref, half_ref, logw_ref,
    q_ref, kp_ref, ko_ref, kn_ref, vp_ref, vo_ref, vn_ref, *refs,
):
    out_ref, prob_ref, bias_ref = refs[-3:]
    cycles, _, lon = bias_ref.shape

    @pl.when(pl.program_id(0) == 0)
    def _():
        fill_bias(first_ref[0], lo_ref, hi_ref, half_ref, logw_ref, bias_ref)

    units = [(pair, i) for pair in range(PPS) for i in range(cycles)]
    keys, values_t = [], []
    for pair in range(PPS):
        c = slice(pair * PAIR, (pair + 1) * PAIR)
        keys.append(jnp.concatenate([kp_ref[0, :, c], ko_ref[:, c], kn_ref[0, :, c]], axis=0))
        values_t.append(jnp.concatenate([vp_ref[0, :, c], vo_ref[:, c], vn_ref[0, :, c]], axis=0).T)

    def scores_of(unit):
        pair, i = unit
        c = slice(pair * PAIR, (pair + 1) * PAIR)
        queries = both_heads(q_ref[i * lon : (i + 1) * lon, c], SCALE)
        bias = bias_ref.at[i]
        chunks = []
        for n in range(SPAN):
            part = dot(keys[pair][(i + n) * lon : (i + n + 1) * lon], queries, ((1,), (1,)))
            b = bias[n * lon : (n + 1) * lon, :]
            chunks.append(part + jnp.concatenate([b, b], axis=1))
        return chunks

    def finish(unit, chunks):
        pair, i = unit
        c = slice(pair * PAIR, (pair + 1) * PAIR)
        peak = chunks[0]
        for n in chunks[1:]:
            peak = jnp.maximum(peak, n)
        peak = jnp.max(peak, axis=0, keepdims=True)
        chunks = [jnp.exp(n - peak) for n in chunks]
        total = chunks[0]
        for n in chunks[1:]:
            total = total + n
        inverse = 1.0 / jnp.sum(total, axis=0, keepdims=True)
        probs = jnp.concatenate([(n * inverse).astype(BF) for n in chunks], axis=0)
        prob_ref[pair, i] = probs
        window = slice(i * lon, (i + SPAN) * lon)
        attended = dot(values_t[pair][:, window], probs, ((1,), (0,)))
        out_ref[i * lon : (i + 1) * lon, c] = own_columns(attended, lon).astype(BF)

    held = scores_of(units[0])
    for n, unit in enumerate(units):
        later = scores_of(units[n + 1]) if n + 1 < len(units) else None
        finish(unit, held)
        held = later


def backward_kernel(
    q_ref, g_ref, o_ref, prob_ref, kp_ref, ko_ref, kn_ref, vp_ref, vo_ref, vn_ref, *refs,
):
    dq_ref, own_key_ref, own_value_ref, low_ref, high_ref = refs[-5:]
    cycles = prob_ref.shape[1]
    lon = prob_ref.shape[2] // SPAN
    units = [(pair, i) for pair in range(PPS) for i in range(cycles)]
    keys_t, values = [], []
    for pair in range(PPS):
        c = slice(pair * PAIR, (pair + 1) * PAIR)
        keys_t.append(jnp.concatenate([kp_ref[0, :, c], ko_ref[:, c], kn_ref[0, :, c]], axis=0).T)
        values.append(jnp.concatenate([vp_ref[0, :, c], vo_ref[:, c], vn_ref[0, :, c]], axis=0))

    def begin(unit):
        pair, i = unit
        c = slice(pair * PAIR, (pair + 1) * PAIR)
        rows = slice(i * lon, (i + 1) * lon)
        grads = both_heads(g_ref[rows, c], 1.0)
        prob_grad = dot(values[pair][i * lon : (i + SPAN) * lon], grads, ((1,), (1,)))
        product = (g_ref[rows, c].astype(F32) * o_ref[rows, c].astype(F32)).T
        row_dot = jnp.concatenate(
            [
                jnp.sum(product[:HEAD_DIM], axis=0, keepdims=True),
                jnp.sum(product[HEAD_DIM:], axis=0, keepdims=True),
            ],
            axis=1,
        )
        return grads, prob_grad, row_dot

    def finish(unit, held):
        pair, i = unit
        grads, prob_grad, row_dot = held
        c = slice(pair * PAIR, (pair + 1) * PAIR)
        rows = slice(i * lon, (i + 1) * lon)
        window = slice(i * lon, (i + SPAN) * lon)
        probs = prob_ref[pair, i]
        value_part = dot(probs, grads, ((1,), (0,)))
        score_grad = (probs.astype(F32) * (prob_grad - row_dot)).astype(BF)
        queries = both_heads(q_ref[rows, c], SCALE)
        key_part = dot(score_grad, queries, ((1,), (0,)))
        query_part = dot(keys_t[pair][:, window], score_grad, ((1,), (0,)))
        dq_ref[rows, c] = (own_columns(query_part, lon) * SCALE).astype(BF)
        return key_part, value_part

    parts = {}
    held = begin(units[0])
    for n, unit in enumerate(units):
        later = begin(units[n + 1]) if n + 1 < len(units) else None
        parts[unit] = finish(unit, held)
        held = later
        if unit[1] == cycles - 1:
            pair = unit[0]
            c = slice(pair * PAIR, (pair + 1) * PAIR)
            for which in range(2):
                near, far = parts[pair, 0][which], parts[pair, 1][which]
                low_ref[which, :lon, c] = near[:lon].astype(BF)
                low_ref[which, lon:, c] = (near[lon : 2 * lon] + far[:lon]).astype(BF)
                own = near[2 * lon : 4 * lon] + far[lon : 3 * lon]
                (own_key_ref, own_value_ref)[which][:, c] = own.astype(BF)
                high_ref[which, :lon, c] = (near[4 * lon :] + far[3 * lon : 4 * lon]).astype(BF)
                high_ref[which, lon:, c] = far[4 * lon :].astype(BF)


def copies_kernel(half, k_ref, v_ref, out_ref, sems):
    width = out_ref.shape[2]
    copies = []
    for which, source in enumerate((k_ref, v_ref)):
        columns = source.at[:, half * width : (half + 1) * width]
        copies.append(pltpu.make_async_copy(columns, out_ref.at[which], sems.at[which]))
    for copy in copies:
        copy.start()
    for copy in copies:
        copy.wait()


def stack_half(half, k, v):
    rows, width = k.shape
    anywhere = pl.BlockSpec(memory_space=pl.ANY)
    return pl.pallas_call(
        functools.partial(copies_kernel, half),
        in_specs=[anywhere] * 2,
        out_specs=anywhere,
        out_shape=jax.ShapeDtypeStruct((2, rows, width // HALVES), BF),
        scratch_shapes=[pltpu.SemaphoreType.DMA((2,))],
        cost_estimate=SMALL,
        name="stack_half",
    )(k, v)


def half_specs(rows, steps, half):
    width = PPS * PAIR
    flat = pl.BlockSpec((rows, width), lambda p: (0, p + half * steps))
    key = pl.BlockSpec((1, rows, width), lambda p: (0, 0, p))
    value = pl.BlockSpec((1, rows, width), lambda p: (1, 0, p))
    both = pl.BlockSpec((2, rows, width), lambda p: (0, 0, p))
    return flat, key, value, both


def forward(half, band, q, k, v, below, above, lon, previous):
    rows, width = q.shape
    cycles = rows // lon
    pairs = width // PAIR // HALVES
    steps = pairs // PPS
    smem = pl.BlockSpec(memory_space=pltpu.SMEM)
    flat, key, value, _ = half_specs(rows, steps, half)
    operands = [*band, q, below, k, above, below, v, above]
    specs = [smem] * len(band) + [flat, key, flat, key, value, flat, value]
    return pl.pallas_call(
        forward_kernel,
        grid=(steps,),
        in_specs=specs + [pl.BlockSpec(memory_space=pl.ANY)] * len(previous),
        out_specs=[flat, pl.BlockSpec((PPS, cycles, SPAN * lon, 2 * lon), lambda p: (p, 0, 0, 0))],
        out_shape=[
            jax.ShapeDtypeStruct((rows, width), BF),
            jax.ShapeDtypeStruct((pairs, cycles, SPAN * lon, 2 * lon), BF),
        ],
        input_output_aliases={len(operands) + n: n for n in range(len(previous))},
        scratch_shapes=[pltpu.VMEM((cycles, SPAN * lon, lon), F32)],
        compiler_params=pltpu.CompilerParams(vmem_limit_bytes=VMEM_LIMIT),
        cost_estimate=LARGE,
        name="attention_forward",
    )(*operands, *previous)


def backward(half, q, g, o, probs, k, v, below, above, lon, previous):
    rows, width = q.shape
    cycles = rows // lon
    pairs = width // PAIR // HALVES
    steps = pairs // PPS
    flat, key, value, both = half_specs(rows, steps, half)
    prob = pl.BlockSpec((PPS, cycles, SPAN * lon, 2 * lon), lambda p: (p, 0, 0, 0))
    whole = jax.ShapeDtypeStruct((rows, width), BF)
    edge = jax.ShapeDtypeStruct((2, rows, width // HALVES), BF)
    operands = [q, g, o, probs, below, k, above, below, v, above]
    specs = [flat, flat, flat, prob, key, flat, key, value, flat, value]
    return pl.pallas_call(
        backward_kernel,
        grid=(steps,),
        in_specs=specs + [pl.BlockSpec(memory_space=pl.ANY)] * len(previous),
        out_specs=[flat, flat, flat, both, both],
        out_shape=[whole, whole, whole, edge, edge],
        input_output_aliases={len(operands) + n: n for n in range(len(previous))},
        compiler_params=pltpu.CompilerParams(vmem_limit_bytes=VMEM_LIMIT),
        cost_estimate=SMALL,
        name="attention_backward",
    )(*operands, *previous)


def total_kernel(below_ref, above_ref, own_key_ref, own_value_ref, key_ref, value_ref):
    for which, (own, out) in enumerate(((own_key_ref, key_ref), (own_value_ref, value_ref))):
        arrived = below_ref[which].astype(F32) + above_ref[which].astype(F32)
        out[...] = (own[...].astype(F32) + arrived).astype(BF)


def add_arrived(half, own_key, own_value, from_below, from_above):
    rows, width = own_key.shape
    steps = width // HALVES // (PPS * PAIR)
    flat, _, _, both = half_specs(rows, steps, half)
    whole = jax.ShapeDtypeStruct((rows, width), BF)
    return pl.pallas_call(
        total_kernel,
        grid=(steps,),
        in_specs=[both, both, flat, flat],
        out_specs=[flat, flat],
        out_shape=[whole, whole],
        input_output_aliases={2: 0, 3: 1},
        cost_estimate=SMALL,
        name="add_arrived",
    )(from_below, from_above, own_key, own_value)


def lat_shift(value, by):
    size = lax.axis_size(LAT)
    pairs = [(i, i + by) for i in range(size) if 0 <= i + by < size]
    return lax.ppermute(value, LAT, pairs)


def core_swap(value):
    return lax.ppermute(value, "core", [(0, 1), (1, 0)])


def after(value, earlier):
    return lax.optimization_barrier((value, earlier))[0]


def copies_of(value, axes):
    return jnp.broadcast_to(value[None], (lax.axis_size(axes),) + value.shape)


def spread(value, axes):
    return lax.all_to_all(copies_of(value, axes), axes, 0, 0, tiled=True)


def scatter_sum(value, axes):
    size = lax.axis_size(axes)
    blocks = value.reshape((size, value.shape[0] // size) + value.shape[1:])
    received = lax.all_to_all(blocks, axes, 0, 0, tiled=True)
    return jnp.sum(received.astype(F32), axis=0)


def local(query_feats, key_feats, value_feats, out_grad, out_proj, cycle_lo, cycle_hi, lon_half):
    cycles, lon, width = query_feats.shape[1:]
    rows = cycles * lon
    total = cycle_lo.shape[0]
    half_width = width // 2
    q = query_feats.reshape(rows, width)
    k = key_feats.reshape(rows, width)
    v = value_feats.reshape(rows, width)
    grad_flat = out_grad.reshape(rows, width)
    core = lax.axis_index("core")
    mine, others = core * half_width, (1 - core) * half_width

    parts = [stack_half(n, k, v) for n in range(HALVES)]
    proj = after(copies_of(out_proj, "y"), parts[0])
    proj = lax.all_to_all(proj, "y", 0, 0, tiled=True).reshape(-1, width)
    parts[1] = after(parts[1], proj)
    below = [lat_shift(part, 1) for part in parts]
    above = [lat_shift(part, -1) for part in parts]
    proj = copies_of(proj, XZ)
    early_q = after(q, proj)
    proj = lax.all_to_all(proj, XZ, 0, 0, tiled=True).reshape(-1, width)

    latitude = (np.arange(total, dtype=np.float32) + np.float32(0.5)) * np.float32(math.pi / total)
    logw = jnp.asarray(np.log(np.sin(latitude)).astype(np.float32))
    first = (lax.axis_index(LAT) * cycles).astype(jnp.int32).reshape(1)
    band = (first, cycle_lo, cycle_hi, lon_half, logw)
    attended, probs = [], []
    for n in range(HALVES):
        out, prob = forward(n, band, early_q, k, v, below[n], above[n], lon, attended)
        attended = [out]
        probs.append(prob)
    attended = attended[0]

    grad_mine = lax.dynamic_slice_in_dim(grad_flat, mine, half_width, axis=1)
    grad_other = lax.dynamic_slice_in_dim(grad_flat, others, half_width, axis=1)
    sent = dot(attended, grad_other, ((0,), (0,))).astype(BF)
    received = core_swap(sent)
    partial = (dot(attended, grad_mine, ((0,), (0,))) + received.astype(F32)).astype(BF)

    proj, partial = lax.optimization_barrier((proj, partial))
    attn_grad = dot(grad_flat, proj, ((1,), (1,))).astype(BF)
    whole, edges = [], []
    for n in range(HALVES):
        *whole, low, high = backward(
            n, q, attn_grad, attended, probs[n], k, v, below[n], above[n], lon, whole
        )
        edges.append((low, high))
    query_grad, key_grad, value_grad = whole

    partial = scatter_sum(partial, XZ).astype(BF)
    partial = scatter_sum(partial, "y").astype(BF)
    edges[-1] = after(edges[-1], partial)
    samples = lax.axis_size(DP)
    gathered = spread(partial, DP).reshape((samples // 2, 2) + partial.shape)
    summed = jnp.sum(gathered.astype(F32), axis=0)
    scaling = 1.0 / math.sqrt(samples * total * lon)
    proj_grad = jnp.concatenate([summed[0], summed[1]], axis=1) * scaling

    for n, (low, high) in enumerate(edges):
        key_grad, value_grad = add_arrived(
            n, key_grad, value_grad, lat_shift(high, 1), lat_shift(low, -1)
        )
    shape = query_feats.shape
    return (
        query_grad.reshape(shape),
        key_grad.reshape(shape),
        value_grad.reshape(shape),
        proj_grad,
    )


def solution(mesh):
    parts = Mesh(mesh.devices.reshape(4, 2, 4, 2, 8), DP + LAT)
    placed = P(DP, LAT, None, None)
    return jax.shard_map(
        local,
        mesh=parts,
        in_specs=(placed, placed, placed, placed, P(LAT, None), P(), P(), P()),
        out_specs=(placed, placed, placed, P(LAT, None)),
        check_vma=False,
    )
```

```python
import math

import jax
import jax.numpy as jnp
import numpy as np
from jax import lax
from jax.experimental import pallas as pl
from jax.experimental.pallas import tpu as pltpu
from jax.sharding import Mesh
from jax.sharding import PartitionSpec as P

HEADS = 16
HEAD_DIM = 64
REACH = 2
PAIR = 2 * HEAD_DIM
PPS = 2
HALVES = 2
SCALE = 1.0 / math.sqrt(HEAD_DIM)
SPAN = 2 * REACH + 1
DP = ("zh", "core")
ZY = ("zl", "y")
LAT = ("x", "zl", "y")
BF = jnp.bfloat16
F32 = jnp.float32
VMEM_LIMIT = 60 * 1024 * 1024
LARGE = pl.CostEstimate(flops=2*10**10, bytes_accessed=4*10**7, transcendentals=0)
SMALL = pl.CostEstimate(flops=10**6, bytes_accessed=10**5, transcendentals=0)


def dot(a, b, dims):
    return lax.dot_general(a, b, (dims, ((), ())), preferred_element_type=F32)


def fill_bias(first, lo_ref, hi_ref, half_ref, logw_ref, bias_ref):
    cycles, _, lon = bias_ref.shape
    total = lo_ref.shape[0]
    key_lon = lax.broadcasted_iota(jnp.int32, (lon, lon), 0)
    query_lon = lax.broadcasted_iota(jnp.int32, (lon, lon), 1)
    gap = jnp.abs(key_lon - query_lon)
    dist = jnp.minimum(gap, lon - gap)
    for i in range(cycles):
        cycle = first + i
        lon_ok = dist <= half_ref[cycle]
        for c in range(SPAN):
            key_cycle = cycle - REACH + c
            ok = (key_cycle >= lo_ref[cycle]) & (key_cycle <= hi_ref[cycle])
            weight = logw_ref[jnp.clip(key_cycle, 0, total - 1)]
            value = jnp.where(ok, weight, -jnp.inf)
            bias_ref[i, c * lon : (c + 1) * lon, :] = jnp.where(lon_ok, value, -jnp.inf)


def head_masks(scale):
    lane = lax.broadcasted_iota(jnp.int32, (1, PAIR), 1)
    first = jnp.where(lane < HEAD_DIM, scale, 0.0).astype(F32)
    return first, scale - first


def both_heads(rows, scale):
    first, second = head_masks(scale)
    wide = rows.astype(F32)
    return jnp.concatenate([(wide * first).astype(BF), (wide * second).astype(BF)], axis=0)


def own_columns(both, lon):
    return jnp.concatenate([both[:HEAD_DIM, :lon], both[HEAD_DIM:, lon:]], axis=0).T


def forward_kernel(
    first_ref, lo_ref, hi_ref, half_ref, logw_ref,
    q_ref, kp_ref, ko_ref, kn_ref, vp_ref, vo_ref, vn_ref, *refs,
):
    out_ref, prob_ref, bias_ref = refs[-3:]
    cycles, _, lon = bias_ref.shape

    @pl.when(pl.program_id(0) == 0)
    def _():
        fill_bias(first_ref[0], lo_ref, hi_ref, half_ref, logw_ref, bias_ref)

    units = [(pair, i) for pair in range(PPS) for i in range(cycles)]
    keys, values_t = [], []
    for pair in range(PPS):
        c = slice(pair * PAIR, (pair + 1) * PAIR)
        keys.append(jnp.concatenate([kp_ref[0, :, c], ko_ref[:, c], kn_ref[0, :, c]], axis=0))
        values_t.append(jnp.concatenate([vp_ref[0, :, c], vo_ref[:, c], vn_ref[0, :, c]], axis=0).T)

    def scores_of(unit):
        pair, i = unit
        c = slice(pair * PAIR, (pair + 1) * PAIR)
        queries = both_heads(q_ref[i * lon : (i + 1) * lon, c], SCALE)
        bias = bias_ref.at[i]
        chunks = []
        for n in range(SPAN):
            part = dot(keys[pair][(i + n) * lon : (i + n + 1) * lon], queries, ((1,), (1,)))
            b = bias[n * lon : (n + 1) * lon, :]
            chunks.append(part + jnp.concatenate([b, b], axis=1))
        return chunks

    def finish(unit, chunks):
        pair, i = unit
        c = slice(pair * PAIR, (pair + 1) * PAIR)
        peak = chunks[0]
        for n in chunks[1:]:
            peak = jnp.maximum(peak, n)
        peak = jnp.max(peak, axis=0, keepdims=True)
        chunks = [jnp.exp(n - peak) for n in chunks]
        total = chunks[0]
        for n in chunks[1:]:
            total = total + n
        inverse = 1.0 / jnp.sum(total, axis=0, keepdims=True)
        probs = jnp.concatenate([(n * inverse).astype(BF) for n in chunks], axis=0)
        prob_ref[pair, i] = probs
        window = slice(i * lon, (i + SPAN) * lon)
        attended = dot(values_t[pair][:, window], probs, ((1,), (0,)))
        out_ref[i * lon : (i + 1) * lon, c] = own_columns(attended, lon).astype(BF)

    held = scores_of(units[0])
    for n, unit in enumerate(units):
        later = scores_of(units[n + 1]) if n + 1 < len(units) else None
        finish(unit, held)
        held = later


def backward_kernel(
    q_ref, g_ref, o_ref, prob_ref, kp_ref, ko_ref, kn_ref, vp_ref, vo_ref, vn_ref, *refs,
):
    dq_ref, own_key_ref, own_value_ref, low_ref, high_ref = refs[-5:]
    cycles = prob_ref.shape[1]
    lon = prob_ref.shape[2] // SPAN
    units = [(pair, i) for pair in range(PPS) for i in range(cycles)]
    keys_t, values = [], []
    for pair in range(PPS):
        c = slice(pair * PAIR, (pair + 1) * PAIR)
        keys_t.append(jnp.concatenate([kp_ref[0, :, c], ko_ref[:, c], kn_ref[0, :, c]], axis=0).T)
        values.append(jnp.concatenate([vp_ref[0, :, c], vo_ref[:, c], vn_ref[0, :, c]], axis=0))

    def begin(unit):
        pair, i = unit
        c = slice(pair * PAIR, (pair + 1) * PAIR)
        rows = slice(i * lon, (i + 1) * lon)
        grads = both_heads(g_ref[rows, c], 1.0)
        prob_grad = dot(values[pair][i * lon : (i + SPAN) * lon], grads, ((1,), (1,)))
        product = (g_ref[rows, c].astype(F32) * o_ref[rows, c].astype(F32)).T
        row_dot = jnp.concatenate(
            [
                jnp.sum(product[:HEAD_DIM], axis=0, keepdims=True),
                jnp.sum(product[HEAD_DIM:], axis=0, keepdims=True),
            ],
            axis=1,
        )
        return grads, prob_grad, row_dot

    def finish(unit, held):
        pair, i = unit
        grads, prob_grad, row_dot = held
        c = slice(pair * PAIR, (pair + 1) * PAIR)
        rows = slice(i * lon, (i + 1) * lon)
        window = slice(i * lon, (i + SPAN) * lon)
        probs = prob_ref[pair, i]
        value_part = dot(probs, grads, ((1,), (0,)))
        score_grad = (probs.astype(F32) * (prob_grad - row_dot)).astype(BF)
        queries = both_heads(q_ref[rows, c], SCALE)
        key_part = dot(score_grad, queries, ((1,), (0,)))
        query_part = dot(keys_t[pair][:, window], score_grad, ((1,), (0,)))
        dq_ref[rows, c] = (own_columns(query_part, lon) * SCALE).astype(BF)
        return key_part, value_part

    parts = {}
    held = begin(units[0])
    for n, unit in enumerate(units):
        later = begin(units[n + 1]) if n + 1 < len(units) else None
        parts[unit] = finish(unit, held)
        held = later
        if unit[1] == cycles - 1:
            pair = unit[0]
            c = slice(pair * PAIR, (pair + 1) * PAIR)
            for which in range(2):
                near, far = parts[pair, 0][which], parts[pair, 1][which]
                low_ref[which, :lon, c] = near[:lon].astype(BF)
                low_ref[which, lon:, c] = (near[lon : 2 * lon] + far[:lon]).astype(BF)
                own = near[2 * lon : 4 * lon] + far[lon : 3 * lon]
                (own_key_ref, own_value_ref)[which][:, c] = own.astype(BF)
                high_ref[which, :lon, c] = (near[4 * lon :] + far[3 * lon : 4 * lon]).astype(BF)
                high_ref[which, lon:, c] = far[4 * lon :].astype(BF)


def half_specs(rows, steps, half):
    width = PPS * PAIR
    flat = pl.BlockSpec((rows, width), lambda p: (0, p + half * steps))
    key = pl.BlockSpec((1, rows, width), lambda p: (0, 0, p))
    value = pl.BlockSpec((1, rows, width), lambda p: (1, 0, p))
    both = pl.BlockSpec((2, rows, width), lambda p: (0, 0, p))
    return flat, key, value, both


def forward(half, band, q, k, v, below, above, lon, previous):
    rows, width = q.shape
    cycles = rows // lon
    pairs = width // PAIR // HALVES
    steps = pairs // PPS
    smem = pl.BlockSpec(memory_space=pltpu.SMEM)
    flat, key, value, _ = half_specs(rows, steps, half)
    operands = [*band, q, below, k, above, below, v, above]
    specs = [smem] * len(band) + [flat, key, flat, key, value, flat, value]
    return pl.pallas_call(
        forward_kernel,
        grid=(steps,),
        in_specs=specs + [pl.BlockSpec(memory_space=pl.ANY)] * len(previous),
        out_specs=[flat, pl.BlockSpec((PPS, cycles, SPAN * lon, 2 * lon), lambda p: (p, 0, 0, 0))],
        out_shape=[
            jax.ShapeDtypeStruct((rows, width), BF),
            jax.ShapeDtypeStruct((pairs, cycles, SPAN * lon, 2 * lon), BF),
        ],
        input_output_aliases={len(operands) + n: n for n in range(len(previous))},
        scratch_shapes=[pltpu.VMEM((cycles, SPAN * lon, lon), F32)],
        compiler_params=pltpu.CompilerParams(vmem_limit_bytes=VMEM_LIMIT),
        cost_estimate=LARGE,
        name="attention_forward",
    )(*operands, *previous)


def backward(half, q, g, o, probs, k, v, below, above, lon, previous):
    rows, width = q.shape
    cycles = rows // lon
    pairs = width // PAIR // HALVES
    steps = pairs // PPS
    flat, key, value, both = half_specs(rows, steps, half)
    prob = pl.BlockSpec((PPS, cycles, SPAN * lon, 2 * lon), lambda p: (p, 0, 0, 0))
    whole = jax.ShapeDtypeStruct((rows, width), BF)
    edge = jax.ShapeDtypeStruct((2, rows, width // HALVES), BF)
    operands = [q, g, o, probs, below, k, above, below, v, above]
    specs = [flat, flat, flat, prob, key, flat, key, value, flat, value]
    return pl.pallas_call(
        backward_kernel,
        grid=(steps,),
        in_specs=specs + [pl.BlockSpec(memory_space=pl.ANY)] * len(previous),
        out_specs=[flat, flat, flat, both, both],
        out_shape=[whole, whole, whole, edge, edge],
        input_output_aliases={len(operands) + n: n for n in range(len(previous))},
        compiler_params=pltpu.CompilerParams(vmem_limit_bytes=VMEM_LIMIT),
        cost_estimate=SMALL,
        name="attention_backward",
    )(*operands, *previous)


def total_kernel(below_ref, above_ref, own_key_ref, own_value_ref, key_ref, value_ref):
    for which, (own, out) in enumerate(((own_key_ref, key_ref), (own_value_ref, value_ref))):
        arrived = below_ref[which].astype(F32) + above_ref[which].astype(F32)
        out[...] = (own[...].astype(F32) + arrived).astype(BF)


def add_arrived(half, own_key, own_value, from_below, from_above):
    rows, width = own_key.shape
    steps = width // HALVES // (PPS * PAIR)
    flat, _, _, both = half_specs(rows, steps, half)
    whole = jax.ShapeDtypeStruct((rows, width), BF)
    return pl.pallas_call(
        total_kernel,
        grid=(steps,),
        in_specs=[both, both, flat, flat],
        out_specs=[flat, flat],
        out_shape=[whole, whole],
        input_output_aliases={2: 0, 3: 1},
        cost_estimate=SMALL,
        name="add_arrived",
    )(from_below, from_above, own_key, own_value)


def lat_shift(value, by):
    size = lax.axis_size(LAT)
    pairs = [(i, i + by) for i in range(size) if 0 <= i + by < size]
    return lax.ppermute(value, LAT, pairs)


def core_swap(value):
    return lax.ppermute(value, "core", [(0, 1), (1, 0)])


def copies_of(value, axes):
    return jnp.broadcast_to(value[None], (lax.axis_size(axes),) + value.shape)


def spread(value, axes):
    return lax.all_to_all(copies_of(value, axes), axes, 0, 0, tiled=True)


def scatter_sum(value, axes):
    size = lax.axis_size(axes)
    blocks = value.reshape((size, value.shape[0] // size) + value.shape[1:])
    received = lax.all_to_all(blocks, axes, 0, 0, tiled=True)
    return jnp.sum(received.astype(F32), axis=0)


def local(query_feats, key_feats, value_feats, out_grad, out_proj, cycle_lo, cycle_hi, lon_half):
    cycles, lon, width = query_feats.shape[1:]
    rows = cycles * lon
    total = cycle_lo.shape[0]
    half_width = width // 2
    q = query_feats.reshape(rows, width)
    k = key_feats.reshape(rows, width)
    v = value_feats.reshape(rows, width)
    grad_flat = out_grad.reshape(rows, width)
    core = lax.axis_index("core")
    mine, others = core * half_width, (1 - core) * half_width

    parts = [
        jnp.stack([k[:, n : n + width // HALVES], v[:, n : n + width // HALVES]])
        for n in range(0, width, width // HALVES)
    ]
    below = [lat_shift(part, 1) for part in parts]
    above = [lat_shift(part, -1) for part in parts]
    proj = spread(out_proj, ZY).reshape(-1, width)
    proj = copies_of(proj, "x")
    proj, early_q = lax.optimization_barrier((proj, q))
    proj = lax.all_to_all(proj, "x", 0, 0, tiled=True).reshape(-1, width)

    latitude = (np.arange(total, dtype=np.float32) + np.float32(0.5)) * np.float32(math.pi / total)
    logw = jnp.asarray(np.log(np.sin(latitude)).astype(np.float32))
    first = (lax.axis_index(LAT) * cycles).astype(jnp.int32).reshape(1)
    band = (first, cycle_lo, cycle_hi, lon_half, logw)
    attended, probs = [], []
    for n in range(HALVES):
        out, prob = forward(n, band, early_q, k, v, below[n], above[n], lon, attended)
        attended = [out]
        probs.append(prob)
    attended = attended[0]

    grad_mine = lax.dynamic_slice_in_dim(grad_flat, mine, half_width, axis=1)
    grad_other = lax.dynamic_slice_in_dim(grad_flat, others, half_width, axis=1)
    sent = dot(attended, grad_other, ((0,), (0,))).astype(BF)
    received = core_swap(sent)
    partial = (dot(attended, grad_mine, ((0,), (0,))) + received.astype(F32)).astype(BF)

    proj, partial = lax.optimization_barrier((proj, partial))
    attn_grad = dot(grad_flat, proj, ((1,), (1,))).astype(BF)
    whole, edges = [], []
    for n in range(HALVES):
        *whole, low, high = backward(
            n, q, attn_grad, attended, probs[n], k, v, below[n], above[n], lon, whole
        )
        edges.append((low, high))
    query_grad, key_grad, value_grad = whole

    partial = scatter_sum(partial, "x").astype(BF)
    partial, edges[-1] = lax.optimization_barrier((partial, edges[-1]))
    partial = scatter_sum(partial, ZY).astype(BF)
    partial, edges[-1] = lax.optimization_barrier((partial, edges[-1]))
    samples = lax.axis_size(DP)
    gathered = spread(partial, DP).reshape((samples // 2, 2) + partial.shape)
    summed = jnp.sum(gathered.astype(F32), axis=0)
    scaling = 1.0 / math.sqrt(samples * total * lon)
    proj_grad = jnp.concatenate([summed[0], summed[1]], axis=1) * scaling

    for n, (low, high) in enumerate(edges):
        key_grad, value_grad = add_arrived(
            n, key_grad, value_grad, lat_shift(high, 1), lat_shift(low, -1)
        )
    shape = query_feats.shape
    return (
        query_grad.reshape(shape),
        key_grad.reshape(shape),
        value_grad.reshape(shape),
        proj_grad,
    )


def solution(mesh):
    parts = Mesh(mesh.devices.reshape(4, 2, 4, 2, 8), DP + LAT)
    placed = P(DP, LAT, None, None)
    return jax.shard_map(
        local,
        mesh=parts,
        in_specs=(placed, placed, placed, placed, P(LAT, None), P(), P(), P()),
        out_specs=(placed, placed, placed, P(LAT, None)),
        check_vma=False,
    )
```

```python
import math

import jax
import jax.numpy as jnp
import numpy as np
from jax import lax
from jax.experimental import pallas as pl
from jax.experimental.pallas import tpu as pltpu
from jax.sharding import Mesh
from jax.sharding import PartitionSpec as P

HEADS = 16
HEAD_DIM = 64
REACH = 2
PAIR = 2 * HEAD_DIM
PPS = 2
HALVES = 2
SCALE = 1.0 / math.sqrt(HEAD_DIM)
SPAN = 2 * REACH + 1
DP = ("zh", "core")
ZY = ("zl", "y")
LAT = ("x", "zl", "y")
BF = jnp.bfloat16
F32 = jnp.float32
VMEM_LIMIT = 60*1024*1024
LARGE = pl.CostEstimate(flops=2*10**10, bytes_accessed=4*10**7, transcendentals=0)
SMALL = pl.CostEstimate(flops=10**6, bytes_accessed=10**5, transcendentals=0)


def dot(a, b, dims):
    return lax.dot_general(a, b, (dims, ((), ())), preferred_element_type=F32)


def fill_bias(first, lo_ref, hi_ref, half_ref, logw_ref, bias_ref):
    cycles, _, lon = bias_ref.shape
    total = lo_ref.shape[0]
    key_lon = lax.broadcasted_iota(jnp.int32, (lon, lon), 0)
    query_lon = lax.broadcasted_iota(jnp.int32, (lon, lon), 1)
    gap = jnp.abs(key_lon - query_lon)
    dist = jnp.minimum(gap, lon - gap)
    for i in range(cycles):
        cycle = first + i
        lon_ok = dist <= half_ref[cycle]
        for c in range(SPAN):
            key_cycle = cycle - REACH + c
            ok = (key_cycle >= lo_ref[cycle]) & (key_cycle <= hi_ref[cycle])
            weight = logw_ref[jnp.clip(key_cycle, 0, total - 1)]
            value = jnp.where(ok, weight, -jnp.inf)
            bias_ref[i, c * lon : (c + 1) * lon, :] = jnp.where(lon_ok, value, -jnp.inf)


def head_masks(scale):
    lane = lax.broadcasted_iota(jnp.int32, (1, PAIR), 1)
    first = jnp.where(lane < HEAD_DIM, scale, 0.0).astype(F32)
    return first, scale - first


def both_heads(rows, scale):
    first, second = head_masks(scale)
    wide = rows.astype(F32)
    return jnp.concatenate([(wide * first).astype(BF), (wide * second).astype(BF)], axis=0)


def own_columns(both, lon):
    return jnp.concatenate([both[:HEAD_DIM, :lon], both[HEAD_DIM:, lon:]], axis=0).T


def forward_kernel(
    first_ref, lo_ref, hi_ref, half_ref, logw_ref,
    q_ref, kp_ref, ko_ref, kn_ref, vp_ref, vo_ref, vn_ref, *refs,
):
    out_ref, prob_ref, bias_ref = refs[-3:]
    cycles, _, lon = bias_ref.shape

    @pl.when(pl.program_id(0) == 0)
    def _():
        fill_bias(first_ref[0], lo_ref, hi_ref, half_ref, logw_ref, bias_ref)

    units = [(pair, i) for pair in range(PPS) for i in range(cycles)]
    keys, values_t = [], []
    for pair in range(PPS):
        c = slice(pair * PAIR, (pair + 1) * PAIR)
        keys.append(jnp.concatenate([kp_ref[0, :, c], ko_ref[:, c], kn_ref[0, :, c]], axis=0))
        values_t.append(jnp.concatenate([vp_ref[0, :, c], vo_ref[:, c], vn_ref[0, :, c]], axis=0).T)

    def scores_of(unit):
        pair, i = unit
        c = slice(pair * PAIR, (pair + 1) * PAIR)
        queries = both_heads(q_ref[i * lon : (i + 1) * lon, c], SCALE)
        bias = bias_ref.at[i]
        chunks = []
        for n in range(SPAN):
            part = dot(keys[pair][(i + n) * lon : (i + n + 1) * lon], queries, ((1,), (1,)))
            b = bias[n * lon : (n + 1) * lon, :]
            chunks.append(part + jnp.concatenate([b, b], axis=1))
        return chunks

    def finish(unit, chunks):
        pair, i = unit
        c = slice(pair * PAIR, (pair + 1) * PAIR)
        peak = chunks[0]
        for n in chunks[1:]:
            peak = jnp.maximum(peak, n)
        peak = jnp.max(peak, axis=0, keepdims=True)
        chunks = [jnp.exp(n - peak) for n in chunks]
        total = chunks[0]
        for n in chunks[1:]:
            total = total + n
        inverse = 1.0 / jnp.sum(total, axis=0, keepdims=True)
        probs = jnp.concatenate([(n * inverse).astype(BF) for n in chunks], axis=0)
        prob_ref[pair, i] = probs
        window = slice(i * lon, (i + SPAN) * lon)
        attended = dot(values_t[pair][:, window], probs, ((1,), (0,)))
        out_ref[i * lon : (i + 1) * lon, c] = own_columns(attended, lon).astype(BF)

    held = scores_of(units[0])
    for n, unit in enumerate(units):
        later = scores_of(units[n + 1]) if n + 1 < len(units) else None
        finish(unit, held)
        held = later


def backward_kernel(
    q_ref, g_ref, o_ref, prob_ref, kp_ref, ko_ref, kn_ref, vp_ref, vo_ref, vn_ref, *refs,
):
    dq_ref, own_key_ref, own_value_ref, low_ref, high_ref = refs[-5:]
    cycles = prob_ref.shape[1]
    lon = prob_ref.shape[2] // SPAN
    units = [(pair, i) for pair in range(PPS) for i in range(cycles)]
    keys_t, values = [], []
    for pair in range(PPS):
        c = slice(pair * PAIR, (pair + 1) * PAIR)
        keys_t.append(jnp.concatenate([kp_ref[0, :, c], ko_ref[:, c], kn_ref[0, :, c]], axis=0).T)
        values.append(jnp.concatenate([vp_ref[0, :, c], vo_ref[:, c], vn_ref[0, :, c]], axis=0))

    def begin(unit):
        pair, i = unit
        c = slice(pair * PAIR, (pair + 1) * PAIR)
        rows = slice(i * lon, (i + 1) * lon)
        grads = both_heads(g_ref[rows, c], 1.0)
        prob_grad = dot(values[pair][i * lon : (i + SPAN) * lon], grads, ((1,), (1,)))
        product = (g_ref[rows, c].astype(F32) * o_ref[rows, c].astype(F32)).T
        row_dot = jnp.concatenate(
            [
                jnp.sum(product[:HEAD_DIM], axis=0, keepdims=True),
                jnp.sum(product[HEAD_DIM:], axis=0, keepdims=True),
            ],
            axis=1,
        )
        return grads, prob_grad, row_dot

    def finish(unit, held):
        pair, i = unit
        grads, prob_grad, row_dot = held
        c = slice(pair * PAIR, (pair + 1) * PAIR)
        rows = slice(i * lon, (i + 1) * lon)
        window = slice(i * lon, (i + SPAN) * lon)
        probs = prob_ref[pair, i]
        value_part = dot(probs, grads, ((1,), (0,)))
        score_grad = (probs.astype(F32) * (prob_grad - row_dot)).astype(BF)
        queries = both_heads(q_ref[rows, c], SCALE)
        key_part = dot(score_grad, queries, ((1,), (0,)))
        query_part = dot(keys_t[pair][:, window], score_grad, ((1,), (0,)))
        dq_ref[rows, c] = (own_columns(query_part, lon) * SCALE).astype(BF)
        return key_part, value_part

    parts = {}
    held = begin(units[0])
    for n, unit in enumerate(units):
        later = begin(units[n + 1]) if n + 1 < len(units) else None
        parts[unit] = finish(unit, held)
        held = later
        if unit[1] == cycles - 1:
            pair = unit[0]
            c = slice(pair * PAIR, (pair + 1) * PAIR)
            for which in range(2):
                near, far = parts[pair, 0][which], parts[pair, 1][which]
                low_ref[which, :lon, c] = near[:lon].astype(BF)
                low_ref[which, lon:, c] = (near[lon : 2 * lon] + far[:lon]).astype(BF)
                own = near[2 * lon : 4 * lon] + far[lon : 3 * lon]
                (own_key_ref, own_value_ref)[which][:, c] = own.astype(BF)
                high_ref[which, :lon, c] = (near[4 * lon :] + far[3 * lon : 4 * lon]).astype(BF)
                high_ref[which, lon:, c] = far[4 * lon :].astype(BF)


def half_specs(rows, steps, half):
    width = PPS * PAIR
    flat = pl.BlockSpec((rows, width), lambda p: (0, p + half * steps))
    key = pl.BlockSpec((1, rows, width), lambda p: (0, 0, p))
    value = pl.BlockSpec((1, rows, width), lambda p: (1, 0, p))
    both = pl.BlockSpec((2, rows, width), lambda p: (0, 0, p))
    return flat, key, value, both


def forward(half, band, q, k, v, below, above, lon, previous):
    rows, width = q.shape
    cycles = rows // lon
    pairs = width // PAIR // HALVES
    steps = pairs // PPS
    smem = pl.BlockSpec(memory_space=pltpu.SMEM)
    flat, key, value, _ = half_specs(rows, steps, half)
    operands = [*band, q, below, k, above, below, v, above]
    specs = [smem] * len(band) + [flat, key, flat, key, value, flat, value]
    return pl.pallas_call(
        forward_kernel,
        grid=(steps,),
        in_specs=specs + [pl.BlockSpec(memory_space=pl.ANY)] * len(previous),
        out_specs=[flat, pl.BlockSpec((PPS, cycles, SPAN * lon, 2 * lon), lambda p: (p, 0, 0, 0))],
        out_shape=[
            jax.ShapeDtypeStruct((rows, width), BF),
            jax.ShapeDtypeStruct((pairs, cycles, SPAN * lon, 2 * lon), BF),
        ],
        input_output_aliases={len(operands) + n: n for n in range(len(previous))},
        scratch_shapes=[pltpu.VMEM((cycles, SPAN * lon, lon), F32)],
        compiler_params=pltpu.CompilerParams(vmem_limit_bytes=VMEM_LIMIT),
        cost_estimate=LARGE,
        name="attention_forward",
    )(*operands, *previous)


def backward(half, q, g, o, probs, k, v, below, above, lon, previous):
    rows, width = q.shape
    cycles = rows // lon
    pairs = width // PAIR // HALVES
    steps = pairs // PPS
    flat, key, value, both = half_specs(rows, steps, half)
    prob = pl.BlockSpec((PPS, cycles, SPAN * lon, 2 * lon), lambda p: (p, 0, 0, 0))
    whole = jax.ShapeDtypeStruct((rows, width), BF)
    edge = jax.ShapeDtypeStruct((2, rows, width // HALVES), BF)
    operands = [q, g, o, probs, below, k, above, below, v, above]
    specs = [flat, flat, flat, prob, key, flat, key, value, flat, value]
    return pl.pallas_call(
        backward_kernel,
        grid=(steps,),
        in_specs=specs + [pl.BlockSpec(memory_space=pl.ANY)] * len(previous),
        out_specs=[flat, flat, flat, both, both],
        out_shape=[whole, whole, whole, edge, edge],
        input_output_aliases={len(operands) + n: n for n in range(len(previous))},
        compiler_params=pltpu.CompilerParams(vmem_limit_bytes=VMEM_LIMIT),
        cost_estimate=SMALL,
        name="attention_backward",
    )(*operands, *previous)


def total_kernel(below_ref, above_ref, own_key_ref, own_value_ref, key_ref, value_ref):
    for which, (own, out) in enumerate(((own_key_ref, key_ref), (own_value_ref, value_ref))):
        arrived = below_ref[which].astype(F32) + above_ref[which].astype(F32)
        out[...] = (own[...].astype(F32) + arrived).astype(BF)


def add_arrived(half, own_key, own_value, from_below, from_above):
    rows, width = own_key.shape
    steps = width // HALVES // (PPS * PAIR)
    flat, _, _, both = half_specs(rows, steps, half)
    whole = jax.ShapeDtypeStruct((rows, width), BF)
    return pl.pallas_call(
        total_kernel,
        grid=(steps,),
        in_specs=[both, both, flat, flat],
        out_specs=[flat, flat],
        out_shape=[whole, whole],
        input_output_aliases={2: 0, 3: 1},
        cost_estimate=SMALL,
        name="add_arrived",
    )(from_below, from_above, own_key, own_value)


def lat_shift(value, by):
    size = lax.axis_size(LAT)
    pairs = [(i, i + by) for i in range(size) if 0 <= i + by < size]
    return lax.ppermute(value, LAT, pairs)


def core_swap(value):
    return lax.ppermute(value, "core", [(0, 1), (1, 0)])


def copies_of(value, axes):
    return jnp.broadcast_to(value[None], (lax.axis_size(axes),) + value.shape)


def spread(value, axes):
    return lax.all_to_all(copies_of(value, axes), axes, 0, 0, tiled=True)


def scatter_sum(value, axes):
    size = lax.axis_size(axes)
    blocks = value.reshape((size, value.shape[0] // size) + value.shape[1:])
    received = lax.all_to_all(blocks, axes, 0, 0, tiled=True)
    return jnp.sum(received.astype(F32), axis=0)


def local(query_feats, key_feats, value_feats, out_grad, out_proj, cycle_lo, cycle_hi, lon_half):
    cycles, lon, width = query_feats.shape[1:]
    rows = cycles * lon
    total = cycle_lo.shape[0]
    half_width = width // 2
    q = query_feats.reshape(rows, width)
    k = key_feats.reshape(rows, width)
    v = value_feats.reshape(rows, width)
    grad_flat = out_grad.reshape(rows, width)
    core = lax.axis_index("core")
    mine, others = core * half_width, (1 - core) * half_width

    parts = [
        jnp.stack([k[:, n : n + width // HALVES], v[:, n : n + width // HALVES]])
        for n in range(0, width, width // HALVES)
    ]
    below = [lat_shift(part, 1) for part in parts]
    above = [lat_shift(part, -1) for part in parts]
    proj = lax.dynamic_slice_in_dim(out_proj, mine, half_width, axis=1)
    proj = spread(proj, ZY).reshape(-1, half_width)
    proj = copies_of(proj, "x")
    proj, early_q = lax.optimization_barrier((proj, q))
    proj = lax.all_to_all(proj, "x", 0, 0, tiled=True).reshape(-1, half_width)

    latitude = (np.arange(total, dtype=np.float32) + np.float32(0.5)) * np.float32(math.pi / total)
    logw = jnp.asarray(np.log(np.sin(latitude)).astype(np.float32))
    first = (lax.axis_index(LAT) * cycles).astype(jnp.int32).reshape(1)
    band = (first, cycle_lo, cycle_hi, lon_half, logw)
    attended, probs = [], []
    for n in range(HALVES):
        out, prob = forward(n, band, early_q, k, v, below[n], above[n], lon, attended)
        attended = [out]
        probs.append(prob)
    attended = attended[0]

    grad_mine = lax.dynamic_slice_in_dim(grad_flat, mine, half_width, axis=1)
    grad_other = lax.dynamic_slice_in_dim(grad_flat, others, half_width, axis=1)
    sent = dot(attended, grad_other, ((0,), (0,))).astype(BF)
    proj, sent = lax.optimization_barrier((proj, sent))
    received = core_swap(sent)
    proj_other = core_swap(proj)
    partial = (dot(attended, grad_mine, ((0,), (0,))) + received.astype(F32)).astype(BF)
    attn_grad = dot(grad_mine, proj, ((1,), (1,))) + dot(grad_other, proj_other, ((1,), (1,)))
    attn_grad = attn_grad.astype(BF)
    whole, edges = [], []
    for n in range(HALVES):
        *whole, low, high = backward(
            n, q, attn_grad, attended, probs[n], k, v, below[n], above[n], lon, whole
        )
        edges.append((low, high))
    query_grad, key_grad, value_grad = whole

    partial = scatter_sum(partial, "x").astype(BF)
    arrived = [(lat_shift(edges[0][1], 1), lat_shift(edges[0][0], -1))]
    partial, arrived[0], edges[1] = lax.optimization_barrier((partial, arrived[0], edges[1]))
    partial = scatter_sum(partial, ZY).astype(BF)
    arrived.append((lat_shift(edges[1][1], 1), lat_shift(edges[1][0], -1)))
    samples = lax.axis_size(DP)
    gathered = spread(partial, DP).reshape((samples // 2, 2) + partial.shape)
    summed = jnp.sum(gathered.astype(F32), axis=0)
    scaling = 1.0 / math.sqrt(samples * total * lon)
    proj_grad = jnp.concatenate([summed[0], summed[1]], axis=1) * scaling

    for n, (from_below, from_above) in enumerate(arrived):
        key_grad, value_grad = add_arrived(n, key_grad, value_grad, from_below, from_above)
    shape = query_feats.shape
    return (
        query_grad.reshape(shape),
        key_grad.reshape(shape),
        value_grad.reshape(shape),
        proj_grad,
    )


def solution(mesh):
    parts = Mesh(mesh.devices.reshape(4, 2, 4, 2, 8), DP + LAT)
    placed = P(DP, LAT, None, None)
    return jax.shard_map(
        local,
        mesh=parts,
        in_specs=(placed, placed, placed, placed, P(LAT, None), P(), P(), P()),
        out_specs=(placed, placed, placed, P(LAT, None)),
        check_vma=False,
    )
```

```python
import math

import jax
import jax.numpy as jnp
import numpy as np
from jax import lax
from jax.experimental import pallas as pl
from jax.experimental.pallas import tpu as pltpu
from jax.sharding import Mesh
from jax.sharding import PartitionSpec as P

HEADS = 16
HEAD_DIM = 64
REACH = 2
PAIR = 2 * HEAD_DIM
PPS = 2
HALVES = 2
SCALE = 1.0 / math.sqrt(HEAD_DIM)
SPAN = 2 * REACH + 1
DP = ("zh", "core")
ZY = ("zl", "y")
LAT = ("x", "zl", "y")
BF = jnp.bfloat16
F32 = jnp.float32
VMEM_LIMIT = 60*1024*1024
SUM_LIMIT = 8 * 1024 * 1024
SMALL = pl.CostEstimate(flops=10**6, bytes_accessed=10**5, transcendentals=0)


def dot(a, b, dims):
    return lax.dot_general(a, b, (dims, ((), ())), preferred_element_type=F32)


def fill_bias(first, lo_ref, hi_ref, half_ref, logw_ref, bias_ref):
    cycles, _, lon = bias_ref.shape
    total = lo_ref.shape[0]
    key_lon = lax.broadcasted_iota(jnp.int32, (lon, lon), 0)
    query_lon = lax.broadcasted_iota(jnp.int32, (lon, lon), 1)
    gap = jnp.abs(key_lon - query_lon)
    dist = jnp.minimum(gap, lon - gap)
    for i in range(cycles):
        cycle = first + i
        lon_ok = dist <= half_ref[cycle]
        for c in range(SPAN):
            key_cycle = cycle - REACH + c
            ok = (key_cycle >= lo_ref[cycle]) & (key_cycle <= hi_ref[cycle])
            weight = logw_ref[jnp.clip(key_cycle, 0, total - 1)]
            value = jnp.where(ok, weight, -jnp.inf)
            bias_ref[i, c * lon : (c + 1) * lon, :] = jnp.where(lon_ok, value, -jnp.inf)


def head_masks(scale):
    lane = lax.broadcasted_iota(jnp.int32, (1, PAIR), 1)
    first = jnp.where(lane < HEAD_DIM, scale, 0.0).astype(F32)
    return first, scale - first


def both_heads(rows, scale):
    first, second = head_masks(scale)
    wide = rows.astype(F32)
    return jnp.concatenate([(wide * first).astype(BF), (wide * second).astype(BF)], axis=0)


def own_columns(both, lon):
    return jnp.concatenate([both[:HEAD_DIM, :lon], both[HEAD_DIM:, lon:]], axis=0).T


def forward_kernel(
    first_ref, lo_ref, hi_ref, half_ref, logw_ref,
    q_ref, kp_ref, ko_ref, kn_ref, vp_ref, vo_ref, vn_ref, *refs,
):
    out_ref, prob_ref, bias_ref = refs[-3:]
    cycles, _, lon = bias_ref.shape

    @pl.when(pl.program_id(0) == 0)
    def _():
        fill_bias(first_ref[0], lo_ref, hi_ref, half_ref, logw_ref, bias_ref)

    units = [(pair, i) for pair in range(PPS) for i in range(cycles)]
    keys, values_t = [], []
    for pair in range(PPS):
        c = slice(pair * PAIR, (pair + 1) * PAIR)
        keys.append(jnp.concatenate([kp_ref[0, :, c], ko_ref[:, c], kn_ref[0, :, c]], axis=0))
        values_t.append(jnp.concatenate([vp_ref[0, :, c], vo_ref[:, c], vn_ref[0, :, c]], axis=0).T)

    def scores_of(unit):
        pair, i = unit
        c = slice(pair * PAIR, (pair + 1) * PAIR)
        queries = both_heads(q_ref[i * lon : (i + 1) * lon, c], SCALE)
        bias = bias_ref.at[i]
        chunks = []
        for n in range(SPAN):
            part = dot(keys[pair][(i + n) * lon : (i + n + 1) * lon], queries, ((1,), (1,)))
            b = bias[n * lon : (n + 1) * lon, :]
            chunks.append(part + jnp.concatenate([b, b], axis=1))
        return chunks

    def finish(unit, chunks):
        pair, i = unit
        c = slice(pair * PAIR, (pair + 1) * PAIR)
        peak = chunks[0]
        for n in chunks[1:]:
            peak = jnp.maximum(peak, n)
        peak = jnp.max(peak, axis=0, keepdims=True)
        chunks = [jnp.exp(n - peak) for n in chunks]
        total = chunks[0]
        for n in chunks[1:]:
            total = total + n
        inverse = 1.0 / jnp.sum(total, axis=0, keepdims=True)
        probs = jnp.concatenate([(n * inverse).astype(BF) for n in chunks], axis=0)
        prob_ref[pair, i] = probs
        window = slice(i * lon, (i + SPAN) * lon)
        attended = dot(values_t[pair][:, window], probs, ((1,), (0,)))
        out_ref[i * lon : (i + 1) * lon, c] = own_columns(attended, lon).astype(BF)

    held = scores_of(units[0])
    for n, unit in enumerate(units):
        later = scores_of(units[n + 1]) if n + 1 < len(units) else None
        finish(unit, held)
        held = later


def backward_kernel(
    q_ref, g_ref, o_ref, ko_ref, vo_ref,
    prob0_ref, kp0_ref, kn0_ref, vp0_ref, vn0_ref,
    prob1_ref, kp1_ref, kn1_ref, vp1_ref, vn1_ref,
    dq_ref, own_key_ref, own_value_ref, low_ref, high_ref,
):
    step, steps = pl.program_id(0), pl.num_programs(0)
    shared = (q_ref, g_ref, o_ref, ko_ref, vo_ref)
    outs = (dq_ref, own_key_ref, own_value_ref, low_ref, high_ref)

    @pl.when(step < steps // HALVES)
    def _():
        backward_pairs(*shared, prob0_ref, kp0_ref, kn0_ref, vp0_ref, vn0_ref, *outs)

    @pl.when(step >= steps // HALVES)
    def _():
        backward_pairs(*shared, prob1_ref, kp1_ref, kn1_ref, vp1_ref, vn1_ref, *outs)


def backward_pairs(
    q_ref, g_ref, o_ref, ko_ref, vo_ref,
    prob_ref, kp_ref, kn_ref, vp_ref, vn_ref,
    dq_ref, own_key_ref, own_value_ref, low_ref, high_ref,
):
    cycles = prob_ref.shape[1]
    lon = prob_ref.shape[2] // SPAN
    units = [(pair, i) for pair in range(PPS) for i in range(cycles)]
    keys_t, values = [], []
    for pair in range(PPS):
        c = slice(pair * PAIR, (pair + 1) * PAIR)
        keys_t.append(jnp.concatenate([kp_ref[0, :, c], ko_ref[:, c], kn_ref[0, :, c]], axis=0).T)
        values.append(jnp.concatenate([vp_ref[0, :, c], vo_ref[:, c], vn_ref[0, :, c]], axis=0))

    def begin(unit):
        pair, i = unit
        c = slice(pair * PAIR, (pair + 1) * PAIR)
        rows = slice(i * lon, (i + 1) * lon)
        grads = both_heads(g_ref[rows, c], 1.0)
        prob_grad = dot(values[pair][i * lon : (i + SPAN) * lon], grads, ((1,), (1,)))
        product = (g_ref[rows, c].astype(F32) * o_ref[rows, c].astype(F32)).T
        row_dot = jnp.concatenate(
            [
                jnp.sum(product[:HEAD_DIM], axis=0, keepdims=True),
                jnp.sum(product[HEAD_DIM:], axis=0, keepdims=True),
            ],
            axis=1,
        )
        return grads, prob_grad, row_dot

    def finish(unit, held):
        pair, i = unit
        grads, prob_grad, row_dot = held
        c = slice(pair * PAIR, (pair + 1) * PAIR)
        rows = slice(i * lon, (i + 1) * lon)
        window = slice(i * lon, (i + SPAN) * lon)
        probs = prob_ref[pair, i]
        value_part = dot(probs, grads, ((1,), (0,)))
        score_grad = (probs.astype(F32) * (prob_grad - row_dot)).astype(BF)
        queries = both_heads(q_ref[rows, c], SCALE)
        key_part = dot(score_grad, queries, ((1,), (0,)))
        query_part = dot(keys_t[pair][:, window], score_grad, ((1,), (0,)))
        dq_ref[rows, c] = (own_columns(query_part, lon) * SCALE).astype(BF)
        return key_part, value_part

    parts = {}
    held = begin(units[0])
    for n, unit in enumerate(units):
        later = begin(units[n + 1]) if n + 1 < len(units) else None
        parts[unit] = finish(unit, held)
        held = later
        if unit[1] == cycles - 1:
            pair = unit[0]
            c = slice(pair * PAIR, (pair + 1) * PAIR)
            for which in range(2):
                near, far = parts[pair, 0][which], parts[pair, 1][which]
                low_ref[which, :lon, c] = near[:lon].astype(BF)
                low_ref[which, lon:, c] = (near[lon : 2 * lon] + far[:lon]).astype(BF)
                own = near[2 * lon : 4 * lon] + far[lon : 3 * lon]
                (own_key_ref, own_value_ref)[which][:, c] = own.astype(BF)
                high_ref[which, :lon, c] = (near[4 * lon :] + far[3 * lon : 4 * lon]).astype(BF)
                high_ref[which, lon:, c] = far[4 * lon :].astype(BF)


def half_specs(rows, steps, half):
    width = PPS * PAIR
    flat = pl.BlockSpec((rows, width), lambda p: (0, p + half * steps))
    key = pl.BlockSpec((1, rows, width), lambda p: (0, 0, p))
    value = pl.BlockSpec((1, rows, width), lambda p: (1, 0, p))
    return flat, key, value


def forward(half, band, q, k, v, below, above, lon, previous):
    rows, width = q.shape
    cycles = rows // lon
    pairs = width // PAIR // HALVES
    steps = pairs // PPS
    smem = pl.BlockSpec(memory_space=pltpu.SMEM)
    flat, key, value = half_specs(rows, steps, half)
    operands = [*band, q, below, k, above, below, v, above]
    specs = [smem] * len(band) + [flat, key, flat, key, value, flat, value]
    return pl.pallas_call(
        forward_kernel,
        grid=(steps,),
        in_specs=specs + [pl.BlockSpec(memory_space=pl.ANY)] * len(previous),
        out_specs=[flat, pl.BlockSpec((PPS, cycles, SPAN * lon, 2 * lon), lambda p: (p, 0, 0, 0))],
        out_shape=[
            jax.ShapeDtypeStruct((rows, width), BF),
            jax.ShapeDtypeStruct((pairs, cycles, SPAN * lon, 2 * lon), BF),
        ],
        input_output_aliases={len(operands) + n: n for n in range(len(previous))},
        scratch_shapes=[pltpu.VMEM((cycles, SPAN * lon, lon), F32)],
        compiler_params=pltpu.CompilerParams(vmem_limit_bytes=VMEM_LIMIT),
        cost_estimate=SMALL,
        name="attention_forward",
    )(*operands, *previous)


def backward(q, g, o, probs, k, v, below, above, lon):
    rows, width = q.shape
    cycles = rows // lon
    block = PPS * PAIR
    steps = width // block
    flat = pl.BlockSpec((rows, block), lambda p: (0, p))
    both = pl.BlockSpec((2, rows, block), lambda p: (0, 0, p))
    operands, specs = [q, g, o, k, v], [flat] * 5
    for n in range(HALVES):

        def place(p, n=n):
            return jnp.clip(p - n * (steps // HALVES), 0, steps // HALVES - 1)

        key = pl.BlockSpec((1, rows, block), lambda p, place=place: (0, 0, place(p)))
        value = pl.BlockSpec((1, rows, block), lambda p, place=place: (1, 0, place(p)))
        prob = pl.BlockSpec(
            (PPS, cycles, SPAN * lon, 2 * lon), lambda p, place=place: (place(p), 0, 0, 0)
        )
        operands += [probs[n], below[n], above[n], below[n], above[n]]
        specs += [prob, key, key, value, value]
    whole = jax.ShapeDtypeStruct((rows, width), BF)
    edge = jax.ShapeDtypeStruct((2, rows, width), BF)
    return pl.pallas_call(
        backward_kernel,
        grid=(steps,),
        in_specs=specs,
        out_specs=[flat, flat, flat, both, both],
        out_shape=[whole, whole, whole, edge, edge],
        compiler_params=pltpu.CompilerParams(vmem_limit_bytes=VMEM_LIMIT),
        cost_estimate=SMALL,
        name="attention_backward",
    )(*operands)


def total_kernel(below_ref, above_ref, own_key_ref, own_value_ref, key_ref, value_ref):
    for which, (own, out) in enumerate(((own_key_ref, key_ref), (own_value_ref, value_ref))):
        arrived = below_ref[which].astype(F32) + above_ref[which].astype(F32)
        out[...] = (own[...].astype(F32) + arrived).astype(BF)


def add_arrived(own_key, own_value, from_below, from_above):
    rows, width = own_key.shape
    block = width // 2
    flat = pl.BlockSpec((rows, block), lambda p: (0, p))
    both = pl.BlockSpec((2, rows, block), lambda p: (0, 0, p))
    whole = jax.ShapeDtypeStruct((rows, width), BF)
    return pl.pallas_call(
        total_kernel,
        grid=(width // block,),
        in_specs=[both, both, flat, flat],
        out_specs=[flat, flat],
        out_shape=[whole, whole],
        compiler_params=pltpu.CompilerParams(vmem_limit_bytes=SUM_LIMIT),
        cost_estimate=SMALL,
        name="add_arrived",
    )(from_below, from_above, own_key, own_value)


def stack_kernel(k_ref, v_ref, out_ref):
    out_ref[0] = k_ref[...]
    out_ref[1] = v_ref[...]


def stack_half(half, k, v):
    rows, width = k.shape
    flat = pl.BlockSpec((rows, width // HALVES), lambda p: (0, half))
    return pl.pallas_call(
        stack_kernel,
        grid=(1,),
        in_specs=[flat, flat],
        out_specs=pl.BlockSpec((2, rows, width // HALVES), lambda p: (0, 0, 0)),
        out_shape=jax.ShapeDtypeStruct((2, rows, width // HALVES), BF),
        compiler_params=pltpu.CompilerParams(vmem_limit_bytes=VMEM_LIMIT),
        cost_estimate=SMALL,
        name="stack_half",
    )(k, v)


def lat_shift(value, by):
    size = lax.axis_size(LAT)
    pairs = [(i, i + by) for i in range(size) if 0 <= i + by < size]
    return lax.ppermute(value, LAT, pairs)


def core_swap(value):
    return lax.ppermute(value, "core", [(0, 1), (1, 0)])


def copies_of(value, axes):
    return jnp.broadcast_to(value[None], (lax.axis_size(axes),) + value.shape)


def spread(value, axes):
    return lax.all_to_all(copies_of(value, axes), axes, 0, 0, tiled=True)


def scatter_sum(value, axes):
    size = lax.axis_size(axes)
    blocks = value.reshape((size, value.shape[0] // size) + value.shape[1:])
    received = lax.all_to_all(blocks, axes, 0, 0, tiled=True)
    return jnp.sum(received.astype(F32), axis=0)


def local(query_feats, key_feats, value_feats, out_grad, out_proj, cycle_lo, cycle_hi, lon_half):
    cycles, lon, width = query_feats.shape[1:]
    rows = cycles * lon
    total = cycle_lo.shape[0]
    half_width = width // 2
    q = query_feats.reshape(rows, width)
    k = key_feats.reshape(rows, width)
    v = value_feats.reshape(rows, width)
    grad_flat = out_grad.reshape(rows, width)
    core = lax.axis_index("core")
    mine, others = core * half_width, (1 - core) * half_width

    parts = [stack_half(n, k, v) for n in range(HALVES)]
    below = [lat_shift(part, 1) for part in parts]
    above = [lat_shift(part, -1) for part in parts]
    proj = lax.dynamic_slice_in_dim(out_proj, mine, half_width, axis=1)
    proj = spread(proj, ZY).reshape(-1, half_width)
    latitude = (np.arange(total, dtype=np.float32) + np.float32(0.5)) * np.float32(math.pi / total)
    logw = jnp.asarray(np.log(np.sin(latitude)).astype(np.float32))
    first = (lax.axis_index(LAT) * cycles).astype(jnp.int32).reshape(1)
    band = (first, cycle_lo, cycle_hi, lon_half, logw)
    attended, probs_first = forward(0, band, q, k, v, below[0], above[0], lon, [])
    proj, attended = lax.optimization_barrier((proj, attended))
    proj = copies_of(proj, "x")
    proj, later_q = lax.optimization_barrier((proj, q))
    proj = lax.all_to_all(proj, "x", 0, 0, tiled=True).reshape(-1, half_width)
    attended, probs_second = forward(
        1, band, later_q, k, v, below[1], above[1], lon, [attended]
    )
    probs = (probs_first, probs_second)

    grad_mine = lax.dynamic_slice_in_dim(grad_flat, mine, half_width, axis=1)
    grad_other = lax.dynamic_slice_in_dim(grad_flat, others, half_width, axis=1)
    sent = dot(attended, grad_other, ((0,), (0,))).astype(BF)
    proj, sent = lax.optimization_barrier((proj, sent))
    received = core_swap(sent)
    proj_other = core_swap(proj)
    partial = (dot(attended, grad_mine, ((0,), (0,))) + received.astype(F32)).astype(BF)
    attn_grad = dot(grad_mine, proj, ((1,), (1,))) + dot(grad_other, proj_other, ((1,), (1,)))
    attn_grad = attn_grad.astype(BF)
    query_grad, own_key, own_value, low, high = backward(
        q, attn_grad, attended, probs, k, v, below, above, lon
    )
    partial = scatter_sum(partial, "x").astype(BF)
    partial, low, high = lax.optimization_barrier((partial, low, high))
    partial = scatter_sum(partial, ZY).astype(BF)
    from_below, from_above = lat_shift(high, 1), lat_shift(low, -1)
    samples = lax.axis_size(DP)
    gathered = spread(partial, DP).reshape((samples // 2, 2) + partial.shape)
    summed = jnp.sum(gathered.astype(F32), axis=0)
    scaling = 1.0 / math.sqrt(samples * total * lon)
    proj_grad = jnp.concatenate([summed[0], summed[1]], axis=1) * scaling

    key_grad, value_grad = add_arrived(own_key, own_value, from_below, from_above)
    shape = query_feats.shape
    return (
        query_grad.reshape(shape),
        key_grad.reshape(shape),
        value_grad.reshape(shape),
        proj_grad,
    )


def solution(mesh):
    parts = Mesh(mesh.devices.reshape(4, 2, 4, 2, 8), DP + LAT)
    placed = P(DP, LAT, None, None)
    return jax.shard_map(
        local,
        mesh=parts,
        in_specs=(placed, placed, placed, placed, P(LAT, None), P(), P(), P()),
        out_specs=(placed, placed, placed, P(LAT, None)),
        check_vma=False,
    )
```

```python
import math

import jax
import jax.numpy as jnp
import numpy as np
from jax import lax
from jax.experimental import pallas as pl
from jax.experimental.pallas import tpu as pltpu
from jax.sharding import Mesh
from jax.sharding import PartitionSpec as P

HEADS = 16
HEAD_DIM = 64
REACH = 2
PAIR = 2 * HEAD_DIM
PPS = 2
HALVES = 2
SCALE = 1.0 / math.sqrt(HEAD_DIM)
SPAN = 2 * REACH + 1
DP = ("zh", "core")
ZY = ("zl", "y")
LAT = ("x", "zl", "y")
BF = jnp.bfloat16
F32 = jnp.float32
VMEM_LIMIT = 60*1024*1024
SUM_LIMIT = 8 * 1024 * 1024
LARGE = pl.CostEstimate(flops=2*10**10, bytes_accessed=4*10**7, transcendentals=0)
SMALL = pl.CostEstimate(flops=10**6, bytes_accessed=10**5, transcendentals=0)


def dot(a, b, dims):
    return lax.dot_general(a, b, (dims, ((), ())), preferred_element_type=F32)


def fill_bias(first, lo_ref, hi_ref, half_ref, logw_ref, bias_ref):
    cycles, _, lon = bias_ref.shape
    total = lo_ref.shape[0]
    key_lon = lax.broadcasted_iota(jnp.int32, (lon, lon), 0)
    query_lon = lax.broadcasted_iota(jnp.int32, (lon, lon), 1)
    gap = jnp.abs(key_lon - query_lon)
    dist = jnp.minimum(gap, lon - gap)
    for i in range(cycles):
        cycle = first + i
        lon_ok = dist <= half_ref[cycle]
        for c in range(SPAN):
            key_cycle = cycle - REACH + c
            ok = (key_cycle >= lo_ref[cycle]) & (key_cycle <= hi_ref[cycle])
            weight = logw_ref[jnp.clip(key_cycle, 0, total - 1)]
            value = jnp.where(ok, weight, -jnp.inf)
            bias_ref[i, c * lon : (c + 1) * lon, :] = jnp.where(lon_ok, value, -jnp.inf)


def head_masks(scale):
    lane = lax.broadcasted_iota(jnp.int32, (1, PAIR), 1)
    first = jnp.where(lane < HEAD_DIM, scale, 0.0).astype(F32)
    return first, scale - first


def both_heads(rows, scale):
    first, second = head_masks(scale)
    wide = rows.astype(F32)
    return jnp.concatenate([(wide * first).astype(BF), (wide * second).astype(BF)], axis=0)


def own_columns(both, lon):
    return jnp.concatenate([both[:HEAD_DIM, :lon], both[HEAD_DIM:, lon:]], axis=0).T


def forward_kernel(
    first_ref, lo_ref, hi_ref, half_ref, logw_ref,
    q_ref, kp_ref, ko_ref, kn_ref, vp_ref, vo_ref, vn_ref, *refs,
):
    out_ref, prob_ref, bias_ref = refs[-3:]
    cycles, _, lon = bias_ref.shape

    @pl.when(pl.program_id(0) == 0)
    def _():
        fill_bias(first_ref[0], lo_ref, hi_ref, half_ref, logw_ref, bias_ref)

    units = [(pair, i) for pair in range(PPS) for i in range(cycles)]
    keys, values_t = [], []
    for pair in range(PPS):
        c = slice(pair * PAIR, (pair + 1) * PAIR)
        keys.append(jnp.concatenate([kp_ref[0, :, c], ko_ref[:, c], kn_ref[0, :, c]], axis=0))
        values_t.append(jnp.concatenate([vp_ref[0, :, c], vo_ref[:, c], vn_ref[0, :, c]], axis=0).T)

    def scores_of(unit):
        pair, i = unit
        c = slice(pair * PAIR, (pair + 1) * PAIR)
        queries = both_heads(q_ref[i * lon : (i + 1) * lon, c], SCALE)
        bias = bias_ref.at[i]
        chunks = []
        for n in range(SPAN):
            part = dot(keys[pair][(i + n) * lon : (i + n + 1) * lon], queries, ((1,), (1,)))
            b = bias[n * lon : (n + 1) * lon, :]
            chunks.append(part + jnp.concatenate([b, b], axis=1))
        return chunks

    def finish(unit, chunks):
        pair, i = unit
        c = slice(pair * PAIR, (pair + 1) * PAIR)
        peak = chunks[0]
        for n in chunks[1:]:
            peak = jnp.maximum(peak, n)
        peak = jnp.max(peak, axis=0, keepdims=True)
        chunks = [jnp.exp(n - peak) for n in chunks]
        total = chunks[0]
        for n in chunks[1:]:
            total = total + n
        inverse = 1.0 / jnp.sum(total, axis=0, keepdims=True)
        probs = jnp.concatenate([(n * inverse).astype(BF) for n in chunks], axis=0)
        prob_ref[pair, i] = probs
        window = slice(i * lon, (i + SPAN) * lon)
        attended = dot(values_t[pair][:, window], probs, ((1,), (0,)))
        out_ref[i * lon : (i + 1) * lon, c] = own_columns(attended, lon).astype(BF)

    held = scores_of(units[0])
    for n, unit in enumerate(units):
        later = scores_of(units[n + 1]) if n + 1 < len(units) else None
        finish(unit, held)
        held = later


def backward_kernel(
    q_ref, g_ref, o_ref, ko_ref, vo_ref,
    prob0_ref, kp0_ref, kn0_ref, vp0_ref, vn0_ref,
    prob1_ref, kp1_ref, kn1_ref, vp1_ref, vn1_ref,
    dq_ref, own_key_ref, own_value_ref, low_ref, high_ref,
):
    step, steps = pl.program_id(0), pl.num_programs(0)
    shared = (q_ref, g_ref, o_ref, ko_ref, vo_ref)
    outs = (dq_ref, own_key_ref, own_value_ref, low_ref, high_ref)

    @pl.when(step < steps // HALVES)
    def _():
        backward_pairs(*shared, prob0_ref, kp0_ref, kn0_ref, vp0_ref, vn0_ref, *outs)

    @pl.when(step >= steps // HALVES)
    def _():
        backward_pairs(*shared, prob1_ref, kp1_ref, kn1_ref, vp1_ref, vn1_ref, *outs)


def backward_pairs(
    q_ref, g_ref, o_ref, ko_ref, vo_ref,
    prob_ref, kp_ref, kn_ref, vp_ref, vn_ref,
    dq_ref, own_key_ref, own_value_ref, low_ref, high_ref,
):
    cycles = prob_ref.shape[1]
    lon = prob_ref.shape[2] // SPAN
    units = [(pair, i) for pair in range(PPS) for i in range(cycles)]
    keys_t, values = [], []
    for pair in range(PPS):
        c = slice(pair * PAIR, (pair + 1) * PAIR)
        keys_t.append(jnp.concatenate([kp_ref[0, :, c], ko_ref[:, c], kn_ref[0, :, c]], axis=0).T)
        values.append(jnp.concatenate([vp_ref[0, :, c], vo_ref[:, c], vn_ref[0, :, c]], axis=0))

    def begin(unit):
        pair, i = unit
        c = slice(pair * PAIR, (pair + 1) * PAIR)
        rows = slice(i * lon, (i + 1) * lon)
        grads = both_heads(g_ref[rows, c], 1.0)
        prob_grad = dot(values[pair][i * lon : (i + SPAN) * lon], grads, ((1,), (1,)))
        product = (g_ref[rows, c].astype(F32) * o_ref[rows, c].astype(F32)).T
        row_dot = jnp.concatenate(
            [
                jnp.sum(product[:HEAD_DIM], axis=0, keepdims=True),
                jnp.sum(product[HEAD_DIM:], axis=0, keepdims=True),
            ],
            axis=1,
        )
        return grads, prob_grad, row_dot

    def finish(unit, held):
        pair, i = unit
        grads, prob_grad, row_dot = held
        c = slice(pair * PAIR, (pair + 1) * PAIR)
        rows = slice(i * lon, (i + 1) * lon)
        window = slice(i * lon, (i + SPAN) * lon)
        probs = prob_ref[pair, i]
        value_part = dot(probs, grads, ((1,), (0,)))
        score_grad = (probs.astype(F32) * (prob_grad - row_dot)).astype(BF)
        queries = both_heads(q_ref[rows, c], SCALE)
        key_part = dot(score_grad, queries, ((1,), (0,)))
        query_part = dot(keys_t[pair][:, window], score_grad, ((1,), (0,)))
        dq_ref[rows, c] = (own_columns(query_part, lon) * SCALE).astype(BF)
        return key_part, value_part

    parts = {}
    held = begin(units[0])
    for n, unit in enumerate(units):
        later = begin(units[n + 1]) if n + 1 < len(units) else None
        parts[unit] = finish(unit, held)
        held = later
        if unit[1] == cycles - 1:
            pair = unit[0]
            c = slice(pair * PAIR, (pair + 1) * PAIR)
            for which in range(2):
                near, far = parts[pair, 0][which], parts[pair, 1][which]
                low_ref[which, :lon, c] = near[:lon].astype(BF)
                low_ref[which, lon:, c] = (near[lon : 2 * lon] + far[:lon]).astype(BF)
                own = near[2 * lon : 4 * lon] + far[lon : 3 * lon]
                (own_key_ref, own_value_ref)[which][:, c] = own.astype(BF)
                high_ref[which, :lon, c] = (near[4 * lon :] + far[3 * lon : 4 * lon]).astype(BF)
                high_ref[which, lon:, c] = far[4 * lon :].astype(BF)


def half_specs(rows, steps, half):
    width = PPS * PAIR
    flat = pl.BlockSpec((rows, width), lambda p: (0, p + half * steps))
    key = pl.BlockSpec((1, rows, width), lambda p: (0, 0, p))
    value = pl.BlockSpec((1, rows, width), lambda p: (1, 0, p))
    return flat, key, value


def forward(half, band, q, k, v, below, above, lon, previous):
    rows, width = q.shape
    cycles = rows // lon
    pairs = width // PAIR // HALVES
    steps = pairs // PPS
    smem = pl.BlockSpec(memory_space=pltpu.SMEM)
    flat, key, value = half_specs(rows, steps, half)
    operands = [*band, q, below, k, above, below, v, above]
    specs = [smem] * len(band) + [flat, key, flat, key, value, flat, value]
    return pl.pallas_call(
        forward_kernel,
        grid=(steps,),
        in_specs=specs + [pl.BlockSpec(memory_space=pl.ANY)] * len(previous),
        out_specs=[flat, pl.BlockSpec((PPS, cycles, SPAN * lon, 2 * lon), lambda p: (p, 0, 0, 0))],
        out_shape=[
            jax.ShapeDtypeStruct((rows, width), BF),
            jax.ShapeDtypeStruct((pairs, cycles, SPAN * lon, 2 * lon), BF),
        ],
        input_output_aliases={len(operands) + n: n for n in range(len(previous))},
        scratch_shapes=[pltpu.VMEM((cycles, SPAN * lon, lon), F32)],
        compiler_params=pltpu.CompilerParams(vmem_limit_bytes=VMEM_LIMIT),
        cost_estimate=LARGE,
        name="attention_forward",
    )(*operands, *previous)


def backward(q, g, o, probs, k, v, below, above, lon):
    rows, width = q.shape
    cycles = rows // lon
    block = PPS * PAIR
    steps = width // block
    flat = pl.BlockSpec((rows, block), lambda p: (0, p))
    both = pl.BlockSpec((2, rows, block), lambda p: (0, 0, p))
    operands, specs = [q, g, o, k, v], [flat] * 5
    for n in range(HALVES):

        def place(p, n=n):
            return jnp.clip(p - n * (steps // HALVES), 0, steps // HALVES - 1)

        key = pl.BlockSpec((1, rows, block), lambda p, place=place: (0, 0, place(p)))
        value = pl.BlockSpec((1, rows, block), lambda p, place=place: (1, 0, place(p)))
        prob = pl.BlockSpec(
            (PPS, cycles, SPAN * lon, 2 * lon), lambda p, place=place: (place(p), 0, 0, 0)
        )
        operands += [probs[n], below[n], above[n], below[n], above[n]]
        specs += [prob, key, key, value, value]
    whole = jax.ShapeDtypeStruct((rows, width), BF)
    edge = jax.ShapeDtypeStruct((2, rows, width), BF)
    return pl.pallas_call(
        backward_kernel,
        grid=(steps,),
        in_specs=specs,
        out_specs=[flat, flat, flat, both, both],
        out_shape=[whole, whole, whole, edge, edge],
        compiler_params=pltpu.CompilerParams(vmem_limit_bytes=VMEM_LIMIT),
        cost_estimate=SMALL,
        name="attention_backward",
    )(*operands)


def total_kernel(below_ref, above_ref, own_key_ref, own_value_ref, key_ref, value_ref):
    for which, (own, out) in enumerate(((own_key_ref, key_ref), (own_value_ref, value_ref))):
        arrived = below_ref[which].astype(F32) + above_ref[which].astype(F32)
        out[...] = (own[...].astype(F32) + arrived).astype(BF)


def add_arrived(own_key, own_value, from_below, from_above):
    rows, width = own_key.shape
    block = width // 2
    flat = pl.BlockSpec((rows, block), lambda p: (0, p))
    both = pl.BlockSpec((2, rows, block), lambda p: (0, 0, p))
    whole = jax.ShapeDtypeStruct((rows, width), BF)
    return pl.pallas_call(
        total_kernel,
        grid=(width // block,),
        in_specs=[both, both, flat, flat],
        out_specs=[flat, flat],
        out_shape=[whole, whole],
        compiler_params=pltpu.CompilerParams(vmem_limit_bytes=SUM_LIMIT),
        cost_estimate=SMALL,
        name="add_arrived",
    )(from_below, from_above, own_key, own_value)


def stack_kernel(k_ref, v_ref, out_ref):
    out_ref[0] = k_ref[...]
    out_ref[1] = v_ref[...]


def stack_half(half, k, v):
    rows, width = k.shape
    flat = pl.BlockSpec((rows, width // HALVES), lambda p: (0, half))
    return pl.pallas_call(
        stack_kernel,
        grid=(1,),
        in_specs=[flat, flat],
        out_specs=pl.BlockSpec((2, rows, width // HALVES), lambda p: (0, 0, 0)),
        out_shape=jax.ShapeDtypeStruct((2, rows, width // HALVES), BF),
        compiler_params=pltpu.CompilerParams(vmem_limit_bytes=VMEM_LIMIT),
        cost_estimate=SMALL,
        name="stack_half",
    )(k, v)


def lat_shift(value, by):
    size = lax.axis_size(LAT)
    pairs = [(i, i + by) for i in range(size) if 0 <= i + by < size]
    return lax.ppermute(value, LAT, pairs)


def core_swap(value):
    return lax.ppermute(value, "core", [(0, 1), (1, 0)])


def copies_of(value, axes):
    return jnp.broadcast_to(value[None], (lax.axis_size(axes),) + value.shape)


def spread(value, axes):
    return lax.all_to_all(copies_of(value, axes), axes, 0, 0, tiled=True)


def scatter_sum(value, axes):
    size = lax.axis_size(axes)
    blocks = value.reshape((size, value.shape[0] // size) + value.shape[1:])
    received = lax.all_to_all(blocks, axes, 0, 0, tiled=True)
    return jnp.sum(received.astype(F32), axis=0)


def local(query_feats, key_feats, value_feats, out_grad, out_proj, cycle_lo, cycle_hi, lon_half):
    cycles, lon, width = query_feats.shape[1:]
    rows = cycles * lon
    total = cycle_lo.shape[0]
    half_width = width // 2
    q = query_feats.reshape(rows, width)
    k = key_feats.reshape(rows, width)
    v = value_feats.reshape(rows, width)
    grad_flat = out_grad.reshape(rows, width)
    core = lax.axis_index("core")
    mine, others = core * half_width, (1 - core) * half_width

    parts = [stack_half(n, k, v) for n in range(HALVES)]
    below = [lat_shift(part, 1) for part in parts]
    above = [lat_shift(part, -1) for part in parts]
    proj = lax.dynamic_slice_in_dim(out_proj, mine, half_width, axis=1)
    proj = spread(proj, ZY).reshape(-1, half_width)
    proj = copies_of(proj, "x")
    proj, early_q = lax.optimization_barrier((proj, q))
    proj = lax.all_to_all(proj, "x", 0, 0, tiled=True).reshape(-1, half_width)

    latitude = (np.arange(total, dtype=np.float32) + np.float32(0.5)) * np.float32(math.pi / total)
    logw = jnp.asarray(np.log(np.sin(latitude)).astype(np.float32))
    first = (lax.axis_index(LAT) * cycles).astype(jnp.int32).reshape(1)
    band = (first, cycle_lo, cycle_hi, lon_half, logw)
    attended, probs = [], []
    for n in range(HALVES):
        out, prob = forward(n, band, early_q, k, v, below[n], above[n], lon, attended)
        attended = [out]
        probs.append(prob)
    attended = attended[0]

    grad_mine = lax.dynamic_slice_in_dim(grad_flat, mine, half_width, axis=1)
    grad_other = lax.dynamic_slice_in_dim(grad_flat, others, half_width, axis=1)
    sent = dot(attended, grad_other, ((0,), (0,))).astype(BF)
    proj, sent = lax.optimization_barrier((proj, sent))
    received = core_swap(sent)
    proj_other = core_swap(proj)
    partial = (dot(attended, grad_mine, ((0,), (0,))) + received.astype(F32)).astype(BF)
    attn_grad = dot(grad_mine, proj, ((1,), (1,))) + dot(grad_other, proj_other, ((1,), (1,)))
    attn_grad = attn_grad.astype(BF)
    query_grad, own_key, own_value, low, high = backward(
        q, attn_grad, attended, probs, k, v, below, above, lon
    )
    partial = scatter_sum(partial, "x").astype(BF)
    partial = scatter_sum(partial, ZY).astype(BF)
    from_below, from_above = lat_shift(high, 1), lat_shift(low, -1)
    samples = lax.axis_size(DP)
    gathered = spread(partial, DP).reshape((samples // 2, 2) + partial.shape)
    summed = jnp.sum(gathered.astype(F32), axis=0)
    scaling = 1.0 / math.sqrt(samples * total * lon)
    proj_grad = jnp.concatenate([summed[0], summed[1]], axis=1) * scaling

    key_grad, value_grad = add_arrived(own_key, own_value, from_below, from_above)
    shape = query_feats.shape
    return (
        query_grad.reshape(shape),
        key_grad.reshape(shape),
        value_grad.reshape(shape),
        proj_grad,
    )


def solution(mesh):
    parts = Mesh(mesh.devices.reshape(4, 2, 4, 2, 8), DP + LAT)
    placed = P(DP, LAT, None, None)
    return jax.shard_map(
        local,
        mesh=parts,
        in_specs=(placed, placed, placed, placed, P(LAT, None), P(), P(), P()),
        out_specs=(placed, placed, placed, P(LAT, None)),
        check_vma=False,
    )
```

```python
import math

import jax
import jax.numpy as jnp
import numpy as np
from jax import lax
from jax.experimental import pallas as pl
from jax.experimental.pallas import tpu as pltpu
from jax.sharding import Mesh
from jax.sharding import PartitionSpec as P

HEADS = 16
HEAD_DIM = 64
REACH = 2
PAIR = 2 * HEAD_DIM
PPS = 2
HALVES = 2
SCALE = 1.0 / math.sqrt(HEAD_DIM)
SPAN = 2 * REACH + 1
DP = ("zh", "core")
ZY = ("zl", "y")
LAT = ("x", "zl", "y")
BF = jnp.bfloat16
F32 = jnp.float32
VMEM_LIMIT = 60*1024*1024
LARGE = pl.CostEstimate(flops=2*10**10, bytes_accessed=4*10**7, transcendentals=0)
SMALL = pl.CostEstimate(flops=10**6, bytes_accessed=10**5, transcendentals=0)


def dot(a, b, dims):
    return lax.dot_general(a, b, (dims, ((), ())), preferred_element_type=F32)


def fill_bias(first, lo_ref, hi_ref, half_ref, logw_ref, bias_ref):
    cycles, _, lon = bias_ref.shape
    total = lo_ref.shape[0]
    key_lon = lax.broadcasted_iota(jnp.int32, (lon, lon), 0)
    query_lon = lax.broadcasted_iota(jnp.int32, (lon, lon), 1)
    gap = jnp.abs(key_lon - query_lon)
    dist = jnp.minimum(gap, lon - gap)
    for i in range(cycles):
        cycle = first + i
        lon_ok = dist <= half_ref[cycle]
        for c in range(SPAN):
            key_cycle = cycle - REACH + c
            ok = (key_cycle >= lo_ref[cycle]) & (key_cycle <= hi_ref[cycle])
            weight = logw_ref[jnp.clip(key_cycle, 0, total - 1)]
            value = jnp.where(ok, weight, -jnp.inf)
            bias_ref[i, c * lon : (c + 1) * lon, :] = jnp.where(lon_ok, value, -jnp.inf)


def head_masks(scale):
    lane = lax.broadcasted_iota(jnp.int32, (1, PAIR), 1)
    first = jnp.where(lane < HEAD_DIM, scale, 0.0).astype(F32)
    return first, scale - first


def both_heads(rows, scale):
    first, second = head_masks(scale)
    wide = rows.astype(F32)
    return jnp.concatenate([(wide * first).astype(BF), (wide * second).astype(BF)], axis=0)


def own_columns(both, lon):
    return jnp.concatenate([both[:HEAD_DIM, :lon], both[HEAD_DIM:, lon:]], axis=0).T


def forward_kernel(
    first_ref, lo_ref, hi_ref, half_ref, logw_ref,
    q_ref, kp_ref, ko_ref, kn_ref, vp_ref, vo_ref, vn_ref, *refs,
):
    out_ref, prob_ref, bias_ref = refs[-3:]
    cycles, _, lon = bias_ref.shape

    @pl.when(pl.program_id(0) == 0)
    def _():
        fill_bias(first_ref[0], lo_ref, hi_ref, half_ref, logw_ref, bias_ref)

    units = [(pair, i) for pair in range(PPS) for i in range(cycles)]
    keys, values_t = [], []
    for pair in range(PPS):
        c = slice(pair * PAIR, (pair + 1) * PAIR)
        keys.append(jnp.concatenate([kp_ref[0, :, c], ko_ref[:, c], kn_ref[0, :, c]], axis=0))
        values_t.append(jnp.concatenate([vp_ref[0, :, c], vo_ref[:, c], vn_ref[0, :, c]], axis=0).T)

    def scores_of(unit):
        pair, i = unit
        c = slice(pair * PAIR, (pair + 1) * PAIR)
        queries = both_heads(q_ref[i * lon : (i + 1) * lon, c], SCALE)
        bias = bias_ref.at[i]
        chunks = []
        for n in range(SPAN):
            part = dot(keys[pair][(i + n) * lon : (i + n + 1) * lon], queries, ((1,), (1,)))
            b = bias[n * lon : (n + 1) * lon, :]
            chunks.append(part + jnp.concatenate([b, b], axis=1))
        return chunks

    def finish(unit, chunks):
        pair, i = unit
        c = slice(pair * PAIR, (pair + 1) * PAIR)
        peak = chunks[0]
        for n in chunks[1:]:
            peak = jnp.maximum(peak, n)
        peak = jnp.max(peak, axis=0, keepdims=True)
        chunks = [jnp.exp(n - peak) for n in chunks]
        total = chunks[0]
        for n in chunks[1:]:
            total = total + n
        inverse = 1.0 / jnp.sum(total, axis=0, keepdims=True)
        probs = jnp.concatenate([(n * inverse).astype(BF) for n in chunks], axis=0)
        prob_ref[pair, i] = probs
        window = slice(i * lon, (i + SPAN) * lon)
        attended = dot(values_t[pair][:, window], probs, ((1,), (0,)))
        out_ref[i * lon : (i + 1) * lon, c] = own_columns(attended, lon).astype(BF)

    held = scores_of(units[0])
    for n, unit in enumerate(units):
        later = scores_of(units[n + 1]) if n + 1 < len(units) else None
        finish(unit, held)
        held = later


def backward_kernel(
    q_ref, g_ref, o_ref, prob_ref, kp_ref, ko_ref, kn_ref, vp_ref, vo_ref, vn_ref, *refs,
):
    dq_ref, own_key_ref, own_value_ref, low_ref, high_ref = refs[-5:]
    cycles = prob_ref.shape[1]
    lon = prob_ref.shape[2] // SPAN
    units = [(pair, i) for pair in range(PPS) for i in range(cycles)]
    keys_t, values = [], []
    for pair in range(PPS):
        c = slice(pair * PAIR, (pair + 1) * PAIR)
        keys_t.append(jnp.concatenate([kp_ref[0, :, c], ko_ref[:, c], kn_ref[0, :, c]], axis=0).T)
        values.append(jnp.concatenate([vp_ref[0, :, c], vo_ref[:, c], vn_ref[0, :, c]], axis=0))

    def begin(unit):
        pair, i = unit
        c = slice(pair * PAIR, (pair + 1) * PAIR)
        rows = slice(i * lon, (i + 1) * lon)
        grads = both_heads(g_ref[rows, c], 1.0)
        prob_grad = dot(values[pair][i * lon : (i + SPAN) * lon], grads, ((1,), (1,)))
        product = (g_ref[rows, c].astype(F32) * o_ref[rows, c].astype(F32)).T
        row_dot = jnp.concatenate(
            [
                jnp.sum(product[:HEAD_DIM], axis=0, keepdims=True),
                jnp.sum(product[HEAD_DIM:], axis=0, keepdims=True),
            ],
            axis=1,
        )
        return grads, prob_grad, row_dot

    def finish(unit, held):
        pair, i = unit
        grads, prob_grad, row_dot = held
        c = slice(pair * PAIR, (pair + 1) * PAIR)
        rows = slice(i * lon, (i + 1) * lon)
        window = slice(i * lon, (i + SPAN) * lon)
        probs = prob_ref[pair, i]
        value_part = dot(probs, grads, ((1,), (0,)))
        score_grad = (probs.astype(F32) * (prob_grad - row_dot)).astype(BF)
        queries = both_heads(q_ref[rows, c], SCALE)
        key_part = dot(score_grad, queries, ((1,), (0,)))
        query_part = dot(keys_t[pair][:, window], score_grad, ((1,), (0,)))
        dq_ref[rows, c] = (own_columns(query_part, lon) * SCALE).astype(BF)
        return key_part, value_part

    parts = {}
    held = begin(units[0])
    for n, unit in enumerate(units):
        later = begin(units[n + 1]) if n + 1 < len(units) else None
        parts[unit] = finish(unit, held)
        held = later
        if unit[1] == cycles - 1:
            pair = unit[0]
            c = slice(pair * PAIR, (pair + 1) * PAIR)
            for which in range(2):
                near, far = parts[pair, 0][which], parts[pair, 1][which]
                low_ref[which, :lon, c] = near[:lon].astype(BF)
                low_ref[which, lon:, c] = (near[lon : 2 * lon] + far[:lon]).astype(BF)
                own = near[2 * lon : 4 * lon] + far[lon : 3 * lon]
                (own_key_ref, own_value_ref)[which][:, c] = own.astype(BF)
                high_ref[which, :lon, c] = (near[4 * lon :] + far[3 * lon : 4 * lon]).astype(BF)
                high_ref[which, lon:, c] = far[4 * lon :].astype(BF)


def half_specs(rows, steps, half):
    width = PPS * PAIR
    flat = pl.BlockSpec((rows, width), lambda p: (0, p + half * steps))
    key = pl.BlockSpec((1, rows, width), lambda p: (0, 0, p))
    value = pl.BlockSpec((1, rows, width), lambda p: (1, 0, p))
    both = pl.BlockSpec((2, rows, width), lambda p: (0, 0, p))
    return flat, key, value, both


def forward(half, band, q, k, v, below, above, lon, previous):
    rows, width = q.shape
    cycles = rows // lon
    pairs = width // PAIR // HALVES
    steps = pairs // PPS
    smem = pl.BlockSpec(memory_space=pltpu.SMEM)
    flat, key, value, _ = half_specs(rows, steps, half)
    operands = [*band, q, below, k, above, below, v, above]
    specs = [smem] * len(band) + [flat, key, flat, key, value, flat, value]
    return pl.pallas_call(
        forward_kernel,
        grid=(steps,),
        in_specs=specs + [pl.BlockSpec(memory_space=pl.ANY)] * len(previous),
        out_specs=[flat, pl.BlockSpec((PPS, cycles, SPAN * lon, 2 * lon), lambda p: (p, 0, 0, 0))],
        out_shape=[
            jax.ShapeDtypeStruct((rows, width), BF),
            jax.ShapeDtypeStruct((pairs, cycles, SPAN * lon, 2 * lon), BF),
        ],
        input_output_aliases={len(operands) + n: n for n in range(len(previous))},
        scratch_shapes=[pltpu.VMEM((cycles, SPAN * lon, lon), F32)],
        compiler_params=pltpu.CompilerParams(vmem_limit_bytes=VMEM_LIMIT),
        cost_estimate=LARGE,
        name="attention_forward",
    )(*operands, *previous)


def backward(half, q, g, o, probs, k, v, below, above, lon, previous):
    rows, width = q.shape
    cycles = rows // lon
    pairs = width // PAIR // HALVES
    steps = pairs // PPS
    flat, key, value, both = half_specs(rows, steps, half)
    prob = pl.BlockSpec((PPS, cycles, SPAN * lon, 2 * lon), lambda p: (p, 0, 0, 0))
    whole = jax.ShapeDtypeStruct((rows, width), BF)
    edge = jax.ShapeDtypeStruct((2, rows, width // HALVES), BF)
    operands = [q, g, o, probs, below, k, above, below, v, above]
    specs = [flat, flat, flat, prob, key, flat, key, value, flat, value]
    return pl.pallas_call(
        backward_kernel,
        grid=(steps,),
        in_specs=specs + [pl.BlockSpec(memory_space=pl.ANY)] * len(previous),
        out_specs=[flat, flat, flat, both, both],
        out_shape=[whole, whole, whole, edge, edge],
        input_output_aliases={len(operands) + n: n for n in range(len(previous))},
        compiler_params=pltpu.CompilerParams(vmem_limit_bytes=VMEM_LIMIT),
        cost_estimate=SMALL,
        name="attention_backward",
    )(*operands, *previous)


def total_kernel(below_ref, above_ref, own_key_ref, own_value_ref, key_ref, value_ref):
    for which, (own, out) in enumerate(((own_key_ref, key_ref), (own_value_ref, value_ref))):
        arrived = below_ref[which].astype(F32) + above_ref[which].astype(F32)
        out[...] = (own[...].astype(F32) + arrived).astype(BF)


def add_arrived(half, own_key, own_value, from_below, from_above):
    rows, width = own_key.shape
    steps = width // HALVES // (PPS * PAIR)
    flat, _, _, both = half_specs(rows, steps, half)
    whole = jax.ShapeDtypeStruct((rows, width), BF)
    return pl.pallas_call(
        total_kernel,
        grid=(steps,),
        in_specs=[both, both, flat, flat],
        out_specs=[flat, flat],
        out_shape=[whole, whole],
        input_output_aliases={2: 0, 3: 1},
        cost_estimate=SMALL,
        name="add_arrived",
    )(from_below, from_above, own_key, own_value)


def lat_shift(value, by):
    size = lax.axis_size(LAT)
    pairs = [(i, i + by) for i in range(size) if 0 <= i + by < size]
    return lax.ppermute(value, LAT, pairs)


def core_swap(value):
    return lax.ppermute(value, "core", [(0, 1), (1, 0)])


def copies_of(value, axes):
    return jnp.broadcast_to(value[None], (lax.axis_size(axes),) + value.shape)


def spread(value, axes):
    return lax.all_to_all(copies_of(value, axes), axes, 0, 0, tiled=True)


def scatter_sum(value, axes):
    size = lax.axis_size(axes)
    blocks = value.reshape((size, value.shape[0] // size) + value.shape[1:])
    received = lax.all_to_all(blocks, axes, 0, 0, tiled=True)
    return jnp.sum(received.astype(F32), axis=0)


def local(query_feats, key_feats, value_feats, out_grad, out_proj, cycle_lo, cycle_hi, lon_half):
    cycles, lon, width = query_feats.shape[1:]
    rows = cycles * lon
    total = cycle_lo.shape[0]
    half_width = width // 2
    q = query_feats.reshape(rows, width)
    k = key_feats.reshape(rows, width)
    v = value_feats.reshape(rows, width)
    grad_flat = out_grad.reshape(rows, width)
    core = lax.axis_index("core")
    mine, others = core * half_width, (1 - core) * half_width

    parts = [
        jnp.stack([k[:, n : n + width // HALVES], v[:, n : n + width // HALVES]])
        for n in range(0, width, width // HALVES)
    ]
    below = [lat_shift(part, 1) for part in parts]
    above = [lat_shift(part, -1) for part in parts]
    proj = lax.dynamic_slice_in_dim(out_proj, mine, half_width, axis=1)
    proj = spread(proj, ZY).reshape(-1, half_width)
    proj = copies_of(proj, "x")
    proj, early_q = lax.optimization_barrier((proj, q))
    proj = lax.all_to_all(proj, "x", 0, 0, tiled=True).reshape(-1, half_width)

    latitude = (np.arange(total, dtype=np.float32) + np.float32(0.5)) * np.float32(math.pi / total)
    logw = jnp.asarray(np.log(np.sin(latitude)).astype(np.float32))
    first = (lax.axis_index(LAT) * cycles).astype(jnp.int32).reshape(1)
    band = (first, cycle_lo, cycle_hi, lon_half, logw)
    attended, probs = [], []
    for n in range(HALVES):
        out, prob = forward(n, band, early_q, k, v, below[n], above[n], lon, attended)
        attended = [out]
        probs.append(prob)
    attended = attended[0]

    grad_mine = lax.dynamic_slice_in_dim(grad_flat, mine, half_width, axis=1)
    grad_other = lax.dynamic_slice_in_dim(grad_flat, others, half_width, axis=1)
    sent = dot(attended, grad_other, ((0,), (0,))).astype(BF)
    received = core_swap(sent)
    proj_other = core_swap(proj)
    partial = (dot(attended, grad_mine, ((0,), (0,))) + received.astype(F32)).astype(BF)
    attn_grad = dot(grad_mine, proj, ((1,), (1,))) + dot(grad_other, proj_other, ((1,), (1,)))
    attn_grad = attn_grad.astype(BF)
    whole, edges = [], []
    for n in range(HALVES):
        *whole, low, high = backward(
            n, q, attn_grad, attended, probs[n], k, v, below[n], above[n], lon, whole
        )
        edges.append((low, high))
    query_grad, key_grad, value_grad = whole

    partial = scatter_sum(partial, "x").astype(BF)
    arrived = [(lat_shift(edges[0][1], 1), lat_shift(edges[0][0], -1))]
    partial, edges[1] = lax.optimization_barrier((partial, edges[1]))
    partial = scatter_sum(partial, ZY).astype(BF)
    partial, arrived[0] = lax.optimization_barrier((partial, arrived[0]))
    arrived.append((lat_shift(edges[1][1], 1), lat_shift(edges[1][0], -1)))
    samples = lax.axis_size(DP)
    gathered = spread(partial, DP).reshape((samples // 2, 2) + partial.shape)
    summed = jnp.sum(gathered.astype(F32), axis=0)
    scaling = 1.0 / math.sqrt(samples * total * lon)
    proj_grad = jnp.concatenate([summed[0], summed[1]], axis=1) * scaling

    for n, (from_below, from_above) in enumerate(arrived):
        key_grad, value_grad = add_arrived(n, key_grad, value_grad, from_below, from_above)
    shape = query_feats.shape
    return (
        query_grad.reshape(shape),
        key_grad.reshape(shape),
        value_grad.reshape(shape),
        proj_grad,
    )


def solution(mesh):
    parts = Mesh(mesh.devices.reshape(4, 2, 4, 2, 8), DP + LAT)
    placed = P(DP, LAT, None, None)
    return jax.shard_map(
        local,
        mesh=parts,
        in_specs=(placed, placed, placed, placed, P(LAT, None), P(), P(), P()),
        out_specs=(placed, placed, placed, P(LAT, None)),
        check_vma=False,
    )
```

```python
import math

import jax
import jax.numpy as jnp
import numpy as np
from jax import lax
from jax.experimental import pallas as pl
from jax.experimental.pallas import tpu as pltpu
from jax.sharding import Mesh
from jax.sharding import PartitionSpec as P

HEADS = 16
HEAD_DIM = 64
REACH = 2
PAIR = 2 * HEAD_DIM
PPS = 2
HALVES = 2
SCALE = 1.0 / math.sqrt(HEAD_DIM)
SPAN = 2 * REACH + 1
DP = ("zh", "core")
ZY = ("zl", "y")
LAT = ("x", "zl", "y")
BF = jnp.bfloat16
F32 = jnp.float32
VMEM_LIMIT = 60*1024*1024
LARGE = pl.CostEstimate(flops=2*10**10, bytes_accessed=4*10**7, transcendentals=0)
SMALL = pl.CostEstimate(flops=10**6, bytes_accessed=10**5, transcendentals=0)


def dot(a, b, dims):
    return lax.dot_general(a, b, (dims, ((), ())), preferred_element_type=F32)


def fill_bias(first, lo_ref, hi_ref, half_ref, logw_ref, bias_ref):
    cycles, _, lon = bias_ref.shape
    total = lo_ref.shape[0]
    key_lon = lax.broadcasted_iota(jnp.int32, (lon, lon), 0)
    query_lon = lax.broadcasted_iota(jnp.int32, (lon, lon), 1)
    gap = jnp.abs(key_lon - query_lon)
    dist = jnp.minimum(gap, lon - gap)
    for i in range(cycles):
        cycle = first + i
        lon_ok = dist <= half_ref[cycle]
        for c in range(SPAN):
            key_cycle = cycle - REACH + c
            ok = (key_cycle >= lo_ref[cycle]) & (key_cycle <= hi_ref[cycle])
            weight = logw_ref[jnp.clip(key_cycle, 0, total - 1)]
            value = jnp.where(ok, weight, -jnp.inf)
            bias_ref[i, c * lon : (c + 1) * lon, :] = jnp.where(lon_ok, value, -jnp.inf)


def head_masks(scale):
    lane = lax.broadcasted_iota(jnp.int32, (1, PAIR), 1)
    first = jnp.where(lane < HEAD_DIM, scale, 0.0).astype(F32)
    return first, scale - first


def both_heads(rows, scale):
    first, second = head_masks(scale)
    wide = rows.astype(F32)
    return jnp.concatenate([(wide * first).astype(BF), (wide * second).astype(BF)], axis=0)


def own_columns(both, lon):
    return jnp.concatenate([both[:HEAD_DIM, :lon], both[HEAD_DIM:, lon:]], axis=0).T


def forward_kernel(
    first_ref, lo_ref, hi_ref, half_ref, logw_ref,
    q_ref, kp_ref, ko_ref, kn_ref, vp_ref, vo_ref, vn_ref, *refs,
):
    out_ref, prob_ref, bias_ref = refs[-3:]
    cycles, _, lon = bias_ref.shape

    @pl.when(pl.program_id(0) == 0)
    def _():
        fill_bias(first_ref[0], lo_ref, hi_ref, half_ref, logw_ref, bias_ref)

    units = [(pair, i) for pair in range(PPS) for i in range(cycles)]
    keys, values_t = [], []
    for pair in range(PPS):
        c = slice(pair * PAIR, (pair + 1) * PAIR)
        keys.append(jnp.concatenate([kp_ref[0, :, c], ko_ref[:, c], kn_ref[0, :, c]], axis=0))
        values_t.append(jnp.concatenate([vp_ref[0, :, c], vo_ref[:, c], vn_ref[0, :, c]], axis=0).T)

    def scores_of(unit):
        pair, i = unit
        c = slice(pair * PAIR, (pair + 1) * PAIR)
        queries = both_heads(q_ref[i * lon : (i + 1) * lon, c], SCALE)
        bias = bias_ref.at[i]
        chunks = []
        for n in range(SPAN):
            part = dot(keys[pair][(i + n) * lon : (i + n + 1) * lon], queries, ((1,), (1,)))
            b = bias[n * lon : (n + 1) * lon, :]
            chunks.append(part + jnp.concatenate([b, b], axis=1))
        return chunks

    def finish(unit, chunks):
        pair, i = unit
        c = slice(pair * PAIR, (pair + 1) * PAIR)
        peak = chunks[0]
        for n in chunks[1:]:
            peak = jnp.maximum(peak, n)
        peak = jnp.max(peak, axis=0, keepdims=True)
        chunks = [jnp.exp(n - peak) for n in chunks]
        total = chunks[0]
        for n in chunks[1:]:
            total = total + n
        inverse = 1.0 / jnp.sum(total, axis=0, keepdims=True)
        probs = jnp.concatenate([(n * inverse).astype(BF) for n in chunks], axis=0)
        prob_ref[pair, i] = probs
        window = slice(i * lon, (i + SPAN) * lon)
        attended = dot(values_t[pair][:, window], probs, ((1,), (0,)))
        out_ref[i * lon : (i + 1) * lon, c] = own_columns(attended, lon).astype(BF)

    held = scores_of(units[0])
    for n, unit in enumerate(units):
        later = scores_of(units[n + 1]) if n + 1 < len(units) else None
        finish(unit, held)
        held = later


def backward_kernel(
    q_ref, g_ref, o_ref, prob_ref, kp_ref, ko_ref, kn_ref, vp_ref, vo_ref, vn_ref, *refs,
):
    dq_ref, own_key_ref, own_value_ref, low_ref, high_ref = refs[-5:]
    cycles = prob_ref.shape[1]
    lon = prob_ref.shape[2] // SPAN
    units = [(pair, i) for pair in range(PPS) for i in range(cycles)]
    keys_t, values = [], []
    for pair in range(PPS):
        c = slice(pair * PAIR, (pair + 1) * PAIR)
        keys_t.append(jnp.concatenate([kp_ref[0, :, c], ko_ref[:, c], kn_ref[0, :, c]], axis=0).T)
        values.append(jnp.concatenate([vp_ref[0, :, c], vo_ref[:, c], vn_ref[0, :, c]], axis=0))

    def begin(unit):
        pair, i = unit
        c = slice(pair * PAIR, (pair + 1) * PAIR)
        rows = slice(i * lon, (i + 1) * lon)
        grads = both_heads(g_ref[rows, c], 1.0)
        prob_grad = dot(values[pair][i * lon : (i + SPAN) * lon], grads, ((1,), (1,)))
        product = (g_ref[rows, c].astype(F32) * o_ref[rows, c].astype(F32)).T
        row_dot = jnp.concatenate(
            [
                jnp.sum(product[:HEAD_DIM], axis=0, keepdims=True),
                jnp.sum(product[HEAD_DIM:], axis=0, keepdims=True),
            ],
            axis=1,
        )
        return grads, prob_grad, row_dot

    def finish(unit, held):
        pair, i = unit
        grads, prob_grad, row_dot = held
        c = slice(pair * PAIR, (pair + 1) * PAIR)
        rows = slice(i * lon, (i + 1) * lon)
        window = slice(i * lon, (i + SPAN) * lon)
        probs = prob_ref[pair, i]
        value_part = dot(probs, grads, ((1,), (0,)))
        score_grad = (probs.astype(F32) * (prob_grad - row_dot)).astype(BF)
        queries = both_heads(q_ref[rows, c], SCALE)
        key_part = dot(score_grad, queries, ((1,), (0,)))
        query_part = dot(keys_t[pair][:, window], score_grad, ((1,), (0,)))
        dq_ref[rows, c] = (own_columns(query_part, lon) * SCALE).astype(BF)
        return key_part, value_part

    parts = {}
    held = begin(units[0])
    for n, unit in enumerate(units):
        later = begin(units[n + 1]) if n + 1 < len(units) else None
        parts[unit] = finish(unit, held)
        held = later
        if unit[1] == cycles - 1:
            pair = unit[0]
            c = slice(pair * PAIR, (pair + 1) * PAIR)
            for which in range(2):
                near, far = parts[pair, 0][which], parts[pair, 1][which]
                low_ref[which, :lon, c] = near[:lon].astype(BF)
                low_ref[which, lon:, c] = (near[lon : 2 * lon] + far[:lon]).astype(BF)
                own = near[2 * lon : 4 * lon] + far[lon : 3 * lon]
                (own_key_ref, own_value_ref)[which][:, c] = own.astype(BF)
                high_ref[which, :lon, c] = (near[4 * lon :] + far[3 * lon : 4 * lon]).astype(BF)
                high_ref[which, lon:, c] = far[4 * lon :].astype(BF)


def half_specs(rows, steps, half):
    width = PPS * PAIR
    flat = pl.BlockSpec((rows, width), lambda p: (0, p + half * steps))
    key = pl.BlockSpec((1, rows, width), lambda p: (0, 0, p))
    value = pl.BlockSpec((1, rows, width), lambda p: (1, 0, p))
    both = pl.BlockSpec((2, rows, width), lambda p: (0, 0, p))
    return flat, key, value, both


def forward(half, band, q, k, v, below, above, lon, previous):
    rows, width = q.shape
    cycles = rows // lon
    pairs = width // PAIR // HALVES
    steps = pairs // PPS
    smem = pl.BlockSpec(memory_space=pltpu.SMEM)
    flat, key, value, _ = half_specs(rows, steps, half)
    operands = [*band, q, below, k, above, below, v, above]
    specs = [smem] * len(band) + [flat, key, flat, key, value, flat, value]
    return pl.pallas_call(
        forward_kernel,
        grid=(steps,),
        in_specs=specs + [pl.BlockSpec(memory_space=pl.ANY)] * len(previous),
        out_specs=[flat, pl.BlockSpec((PPS, cycles, SPAN * lon, 2 * lon), lambda p: (p, 0, 0, 0))],
        out_shape=[
            jax.ShapeDtypeStruct((rows, width), BF),
            jax.ShapeDtypeStruct((pairs, cycles, SPAN * lon, 2 * lon), BF),
        ],
        input_output_aliases={len(operands) + n: n for n in range(len(previous))},
        scratch_shapes=[pltpu.VMEM((cycles, SPAN * lon, lon), F32)],
        compiler_params=pltpu.CompilerParams(vmem_limit_bytes=VMEM_LIMIT),
        cost_estimate=LARGE,
        name="attention_forward",
    )(*operands, *previous)


def backward(half, q, g, o, probs, k, v, below, above, lon, previous):
    rows, width = q.shape
    cycles = rows // lon
    pairs = width // PAIR // HALVES
    steps = pairs // PPS
    flat, key, value, both = half_specs(rows, steps, half)
    prob = pl.BlockSpec((PPS, cycles, SPAN * lon, 2 * lon), lambda p: (p, 0, 0, 0))
    whole = jax.ShapeDtypeStruct((rows, width), BF)
    edge = jax.ShapeDtypeStruct((2, rows, width // HALVES), BF)
    operands = [q, g, o, probs, below, k, above, below, v, above]
    specs = [flat, flat, flat, prob, key, flat, key, value, flat, value]
    return pl.pallas_call(
        backward_kernel,
        grid=(steps,),
        in_specs=specs + [pl.BlockSpec(memory_space=pl.ANY)] * len(previous),
        out_specs=[flat, flat, flat, both, both],
        out_shape=[whole, whole, whole, edge, edge],
        input_output_aliases={len(operands) + n: n for n in range(len(previous))},
        compiler_params=pltpu.CompilerParams(vmem_limit_bytes=VMEM_LIMIT),
        cost_estimate=SMALL,
        name="attention_backward",
    )(*operands, *previous)


def total_kernel(below_ref, above_ref, own_key_ref, own_value_ref, key_ref, value_ref):
    for which, (own, out) in enumerate(((own_key_ref, key_ref), (own_value_ref, value_ref))):
        arrived = below_ref[which].astype(F32) + above_ref[which].astype(F32)
        out[...] = (own[...].astype(F32) + arrived).astype(BF)


def add_arrived(half, own_key, own_value, from_below, from_above):
    rows, width = own_key.shape
    steps = width // HALVES // (PPS * PAIR)
    flat, _, _, both = half_specs(rows, steps, half)
    whole = jax.ShapeDtypeStruct((rows, width), BF)
    return pl.pallas_call(
        total_kernel,
        grid=(steps,),
        in_specs=[both, both, flat, flat],
        out_specs=[flat, flat],
        out_shape=[whole, whole],
        input_output_aliases={2: 0, 3: 1},
        cost_estimate=SMALL,
        name="add_arrived",
    )(from_below, from_above, own_key, own_value)


def lat_shift(value, by):
    size = lax.axis_size(LAT)
    pairs = [(i, i + by) for i in range(size) if 0 <= i + by < size]
    return lax.ppermute(value, LAT, pairs)


def core_swap(value):
    return lax.ppermute(value, "core", [(0, 1), (1, 0)])


def copies_of(value, axes):
    return jnp.broadcast_to(value[None], (lax.axis_size(axes),) + value.shape)


def spread(value, axes):
    return lax.all_to_all(copies_of(value, axes), axes, 0, 0, tiled=True)


def scatter_sum(value, axes):
    size = lax.axis_size(axes)
    blocks = value.reshape((size, value.shape[0] // size) + value.shape[1:])
    received = lax.all_to_all(blocks, axes, 0, 0, tiled=True)
    return jnp.sum(received.astype(F32), axis=0)


def local(query_feats, key_feats, value_feats, out_grad, out_proj, cycle_lo, cycle_hi, lon_half):
    cycles, lon, width = query_feats.shape[1:]
    rows = cycles * lon
    total = cycle_lo.shape[0]
    half_width = width // 2
    q = query_feats.reshape(rows, width)
    k = key_feats.reshape(rows, width)
    v = value_feats.reshape(rows, width)
    grad_flat = out_grad.reshape(rows, width)
    core = lax.axis_index("core")
    mine, others = core * half_width, (1 - core) * half_width

    parts = [
        jnp.stack([k[:, n : n + width // HALVES], v[:, n : n + width // HALVES]])
        for n in range(0, width, width // HALVES)
    ]
    below = [lat_shift(part, 1) for part in parts]
    above = [lat_shift(part, -1) for part in parts]
    proj = lax.dynamic_slice_in_dim(out_proj, mine, half_width, axis=1)
    proj = spread(proj, ZY).reshape(-1, half_width)
    proj = copies_of(proj, "x")
    proj, early_q = lax.optimization_barrier((proj, q))
    proj = lax.all_to_all(proj, "x", 0, 0, tiled=True).reshape(-1, half_width)

    latitude = (np.arange(total, dtype=np.float32) + np.float32(0.5)) * np.float32(math.pi / total)
    logw = jnp.asarray(np.log(np.sin(latitude)).astype(np.float32))
    first = (lax.axis_index(LAT) * cycles).astype(jnp.int32).reshape(1)
    band = (first, cycle_lo, cycle_hi, lon_half, logw)
    attended, probs = [], []
    for n in range(HALVES):
        out, prob = forward(n, band, early_q, k, v, below[n], above[n], lon, attended)
        attended = [out]
        probs.append(prob)
    attended = attended[0]

    grad_mine = lax.dynamic_slice_in_dim(grad_flat, mine, half_width, axis=1)
    grad_other = lax.dynamic_slice_in_dim(grad_flat, others, half_width, axis=1)
    sent = dot(attended, grad_other, ((0,), (0,))).astype(BF)
    received = core_swap(sent)
    proj_other = core_swap(proj)
    partial = (dot(attended, grad_mine, ((0,), (0,))) + received.astype(F32)).astype(BF)
    attn_grad = dot(grad_mine, proj, ((1,), (1,))) + dot(grad_other, proj_other, ((1,), (1,)))
    attn_grad = attn_grad.astype(BF)
    whole, edges = [], []
    for n in range(HALVES):
        *whole, low, high = backward(
            n, q, attn_grad, attended, probs[n], k, v, below[n], above[n], lon, whole
        )
        edges.append((low, high))
    query_grad, key_grad, value_grad = whole

    partial = scatter_sum(partial, "x").astype(BF)
    arrived = [(lat_shift(edges[0][1], 1), lat_shift(edges[0][0], -1))]
    partial = scatter_sum(partial, ZY).astype(BF)
    partial, arrived[0] = lax.optimization_barrier((partial, arrived[0]))
    arrived.append((lat_shift(edges[1][1], 1), lat_shift(edges[1][0], -1)))
    samples = lax.axis_size(DP)
    gathered = spread(partial, DP).reshape((samples // 2, 2) + partial.shape)
    summed = jnp.sum(gathered.astype(F32), axis=0)
    scaling = 1.0 / math.sqrt(samples * total * lon)
    proj_grad = jnp.concatenate([summed[0], summed[1]], axis=1) * scaling

    for n, (from_below, from_above) in enumerate(arrived):
        key_grad, value_grad = add_arrived(n, key_grad, value_grad, from_below, from_above)
    shape = query_feats.shape
    return (
        query_grad.reshape(shape),
        key_grad.reshape(shape),
        value_grad.reshape(shape),
        proj_grad,
    )


def solution(mesh):
    parts = Mesh(mesh.devices.reshape(4, 2, 4, 2, 8), DP + LAT)
    placed = P(DP, LAT, None, None)
    return jax.shard_map(
        local,
        mesh=parts,
        in_specs=(placed, placed, placed, placed, P(LAT, None), P(), P(), P()),
        out_specs=(placed, placed, placed, P(LAT, None)),
        check_vma=False,
    )
```

```python
import math

import jax
import jax.numpy as jnp
import numpy as np
from jax import lax
from jax.experimental import pallas as pl
from jax.experimental.pallas import tpu as pltpu
from jax.sharding import Mesh
from jax.sharding import PartitionSpec as P

HEADS = 16
HEAD_DIM = 64
REACH = 2
PAIR = 2 * HEAD_DIM
PPS = 2
HALVES = 2
SPLIT = 3
SCALE = 1.0 / math.sqrt(HEAD_DIM)
SPAN = 2 * REACH + 1
DP = ("zh", "core")
ZY = ("zl", "y")
LAT = ("x", "zl", "y")
BF = jnp.bfloat16
F32 = jnp.float32
VMEM_LIMIT = 60*1024*1024
LARGE = pl.CostEstimate(flops=2*10**10, bytes_accessed=4*10**7, transcendentals=0)
SMALL = pl.CostEstimate(flops=10**6, bytes_accessed=10**5, transcendentals=0)


def dot(a, b, dims):
    return lax.dot_general(a, b, (dims, ((), ())), preferred_element_type=F32)


def fill_bias(first, lo_ref, hi_ref, half_ref, logw_ref, bias_ref):
    cycles, _, lon = bias_ref.shape
    total = lo_ref.shape[0]
    key_lon = lax.broadcasted_iota(jnp.int32, (lon, lon), 0)
    query_lon = lax.broadcasted_iota(jnp.int32, (lon, lon), 1)
    gap = jnp.abs(key_lon - query_lon)
    dist = jnp.minimum(gap, lon - gap)
    for i in range(cycles):
        cycle = first + i
        lon_ok = dist <= half_ref[cycle]
        for c in range(SPAN):
            key_cycle = cycle - REACH + c
            ok = (key_cycle >= lo_ref[cycle]) & (key_cycle <= hi_ref[cycle])
            weight = logw_ref[jnp.clip(key_cycle, 0, total - 1)]
            value = jnp.where(ok, weight, -jnp.inf)
            bias_ref[i, c * lon : (c + 1) * lon, :] = jnp.where(lon_ok, value, -jnp.inf)


def head_masks(scale):
    lane = lax.broadcasted_iota(jnp.int32, (1, PAIR), 1)
    first = jnp.where(lane < HEAD_DIM, scale, 0.0).astype(F32)
    return first, scale - first


def both_heads(rows, scale):
    first, second = head_masks(scale)
    wide = rows.astype(F32)
    return jnp.concatenate([(wide * first).astype(BF), (wide * second).astype(BF)], axis=0)


def own_columns(both, lon):
    return jnp.concatenate([both[:HEAD_DIM, :lon], both[HEAD_DIM:, lon:]], axis=0).T


def forward_kernel(
    first_ref, lo_ref, hi_ref, half_ref, logw_ref,
    q_ref, kp_ref, ko_ref, kn_ref, vp_ref, vo_ref, vn_ref, *refs,
):
    out_ref, prob_ref, bias_ref = refs[-3:]
    cycles, _, lon = bias_ref.shape

    @pl.when(pl.program_id(0) == 0)
    def _():
        fill_bias(first_ref[0], lo_ref, hi_ref, half_ref, logw_ref, bias_ref)

    units = [(pair, i) for pair in range(PPS) for i in range(cycles)]
    keys, values_t = [], []
    for pair in range(PPS):
        c = slice(pair * PAIR, (pair + 1) * PAIR)
        keys.append(jnp.concatenate([kp_ref[0, :, c], ko_ref[:, c], kn_ref[0, :, c]], axis=0))
        values_t.append(jnp.concatenate([vp_ref[0, :, c], vo_ref[:, c], vn_ref[0, :, c]], axis=0).T)

    def scores_of(unit):
        pair, i = unit
        c = slice(pair * PAIR, (pair + 1) * PAIR)
        queries = both_heads(q_ref[i * lon : (i + 1) * lon, c], SCALE)
        bias = bias_ref.at[i]
        chunks = []
        for n in range(SPAN):
            part = dot(keys[pair][(i + n) * lon : (i + n + 1) * lon], queries, ((1,), (1,)))
            b = bias[n * lon : (n + 1) * lon, :]
            chunks.append(part + jnp.concatenate([b, b], axis=1))
        return chunks

    def finish(unit, chunks):
        pair, i = unit
        c = slice(pair * PAIR, (pair + 1) * PAIR)
        peak = chunks[0]
        for n in chunks[1:]:
            peak = jnp.maximum(peak, n)
        peak = jnp.max(peak, axis=0, keepdims=True)
        chunks = [jnp.exp(n - peak) for n in chunks]
        total = chunks[0]
        for n in chunks[1:]:
            total = total + n
        inverse = 1.0 / jnp.sum(total, axis=0, keepdims=True)
        probs = jnp.concatenate([(n * inverse).astype(BF) for n in chunks], axis=0)
        prob_ref[pair, i] = probs
        window = slice(i * lon, (i + SPAN) * lon)
        attended = dot(values_t[pair][:, window], probs, ((1,), (0,)))
        out_ref[i * lon : (i + 1) * lon, c] = own_columns(attended, lon).astype(BF)

    held = scores_of(units[0])
    for n, unit in enumerate(units):
        later = scores_of(units[n + 1]) if n + 1 < len(units) else None
        finish(unit, held)
        held = later


def backward_kernel(
    q_ref, g_ref, o_ref, prob_ref, kp_ref, ko_ref, kn_ref, vp_ref, vo_ref, vn_ref, *refs,
):
    dq_ref, own_key_ref, own_value_ref, low_ref, high_ref = refs[-5:]
    cycles = prob_ref.shape[1]
    lon = prob_ref.shape[2] // SPAN
    units = [(pair, i) for pair in range(PPS) for i in range(cycles)]
    keys_t, values = [], []
    for pair in range(PPS):
        c = slice(pair * PAIR, (pair + 1) * PAIR)
        keys_t.append(jnp.concatenate([kp_ref[0, :, c], ko_ref[:, c], kn_ref[0, :, c]], axis=0).T)
        values.append(jnp.concatenate([vp_ref[0, :, c], vo_ref[:, c], vn_ref[0, :, c]], axis=0))

    def begin(unit):
        pair, i = unit
        c = slice(pair * PAIR, (pair + 1) * PAIR)
        rows = slice(i * lon, (i + 1) * lon)
        grads = both_heads(g_ref[rows, c], 1.0)
        prob_grad = dot(values[pair][i * lon : (i + SPAN) * lon], grads, ((1,), (1,)))
        product = (g_ref[rows, c].astype(F32) * o_ref[rows, c].astype(F32)).T
        row_dot = jnp.concatenate(
            [
                jnp.sum(product[:HEAD_DIM], axis=0, keepdims=True),
                jnp.sum(product[HEAD_DIM:], axis=0, keepdims=True),
            ],
            axis=1,
        )
        return grads, prob_grad, row_dot

    def finish(unit, held):
        pair, i = unit
        grads, prob_grad, row_dot = held
        c = slice(pair * PAIR, (pair + 1) * PAIR)
        rows = slice(i * lon, (i + 1) * lon)
        window = slice(i * lon, (i + SPAN) * lon)
        probs = prob_ref[pair, i]
        value_part = dot(probs, grads, ((1,), (0,)))
        score_grad = (probs.astype(F32) * (prob_grad - row_dot)).astype(BF)
        queries = both_heads(q_ref[rows, c], SCALE)
        key_part = dot(score_grad, queries, ((1,), (0,)))
        query_part = dot(keys_t[pair][:, window], score_grad, ((1,), (0,)))
        dq_ref[rows, c] = (own_columns(query_part, lon) * SCALE).astype(BF)
        return key_part, value_part

    parts = {}
    held = begin(units[0])
    for n, unit in enumerate(units):
        later = begin(units[n + 1]) if n + 1 < len(units) else None
        parts[unit] = finish(unit, held)
        held = later
        if unit[1] == cycles - 1:
            pair = unit[0]
            c = slice(pair * PAIR, (pair + 1) * PAIR)
            for which in range(2):
                near, far = parts[pair, 0][which], parts[pair, 1][which]
                low_ref[which, :lon, c] = near[:lon].astype(BF)
                low_ref[which, lon:, c] = (near[lon : 2 * lon] + far[:lon]).astype(BF)
                own = near[2 * lon : 4 * lon] + far[lon : 3 * lon]
                (own_key_ref, own_value_ref)[which][:, c] = own.astype(BF)
                high_ref[which, :lon, c] = (near[4 * lon :] + far[3 * lon : 4 * lon]).astype(BF)
                high_ref[which, lon:, c] = far[4 * lon :].astype(BF)


def part_pairs(width):
    pairs = width // PAIR
    first = pairs * SPLIT // 4
    return ((0, first), (first, pairs - first))


def half_specs(rows, begin, half):
    width = PPS * PAIR
    flat = pl.BlockSpec((rows, width), lambda p: (0, p + begin // PPS))
    key = pl.BlockSpec((1, rows, width), lambda p: (0, 0, p))
    value = pl.BlockSpec((1, rows, width), lambda p: (1, 0, p))
    both = pl.BlockSpec((2, rows, width), lambda p: (0, 0, p))
    return flat, key, value, both


def forward(half, band, q, k, v, below, above, lon, previous):
    rows, width = q.shape
    cycles = rows // lon
    begin, pairs = part_pairs(width)[half]
    steps = pairs // PPS
    smem = pl.BlockSpec(memory_space=pltpu.SMEM)
    flat, key, value, _ = half_specs(rows, begin, half)
    operands = [*band, q, below, k, above, below, v, above]
    specs = [smem] * len(band) + [flat, key, flat, key, value, flat, value]
    return pl.pallas_call(
        forward_kernel,
        grid=(steps,),
        in_specs=specs + [pl.BlockSpec(memory_space=pl.ANY)] * len(previous),
        out_specs=[flat, pl.BlockSpec((PPS, cycles, SPAN * lon, 2 * lon), lambda p: (p, 0, 0, 0))],
        out_shape=[
            jax.ShapeDtypeStruct((rows, width), BF),
            jax.ShapeDtypeStruct((pairs, cycles, SPAN * lon, 2 * lon), BF),
        ],
        input_output_aliases={len(operands) + n: n for n in range(len(previous))},
        scratch_shapes=[pltpu.VMEM((cycles, SPAN * lon, lon), F32)],
        compiler_params=pltpu.CompilerParams(vmem_limit_bytes=VMEM_LIMIT),
        cost_estimate=LARGE,
        name="attention_forward",
    )(*operands, *previous)


def backward(half, q, g, o, probs, k, v, below, above, lon, previous):
    rows, width = q.shape
    cycles = rows // lon
    begin, pairs = part_pairs(width)[half]
    steps = pairs // PPS
    flat, key, value, both = half_specs(rows, begin, half)
    prob = pl.BlockSpec((PPS, cycles, SPAN * lon, 2 * lon), lambda p: (p, 0, 0, 0))
    whole = jax.ShapeDtypeStruct((rows, width), BF)
    edge = jax.ShapeDtypeStruct((2, rows, pairs * PAIR), BF)
    operands = [q, g, o, probs, below, k, above, below, v, above]
    specs = [flat, flat, flat, prob, key, flat, key, value, flat, value]
    return pl.pallas_call(
        backward_kernel,
        grid=(steps,),
        in_specs=specs + [pl.BlockSpec(memory_space=pl.ANY)] * len(previous),
        out_specs=[flat, flat, flat, both, both],
        out_shape=[whole, whole, whole, edge, edge],
        input_output_aliases={len(operands) + n: n for n in range(len(previous))},
        compiler_params=pltpu.CompilerParams(vmem_limit_bytes=VMEM_LIMIT),
        cost_estimate=SMALL,
        name="attention_backward",
    )(*operands, *previous)


def total_kernel(below_ref, above_ref, own_key_ref, own_value_ref, key_ref, value_ref):
    for which, (own, out) in enumerate(((own_key_ref, key_ref), (own_value_ref, value_ref))):
        arrived = below_ref[which].astype(F32) + above_ref[which].astype(F32)
        out[...] = (own[...].astype(F32) + arrived).astype(BF)


def add_arrived(half, own_key, own_value, from_below, from_above):
    rows, width = own_key.shape
    begin, pairs = part_pairs(width)[half]
    steps = pairs // PPS
    flat, _, _, both = half_specs(rows, begin, half)
    whole = jax.ShapeDtypeStruct((rows, width), BF)
    return pl.pallas_call(
        total_kernel,
        grid=(steps,),
        in_specs=[both, both, flat, flat],
        out_specs=[flat, flat],
        out_shape=[whole, whole],
        input_output_aliases={2: 0, 3: 1},
        cost_estimate=SMALL,
        name="add_arrived",
    )(from_below, from_above, own_key, own_value)


def lat_shift(value, by):
    size = lax.axis_size(LAT)
    pairs = [(i, i + by) for i in range(size) if 0 <= i + by < size]
    return lax.ppermute(value, LAT, pairs)


def core_swap(value):
    return lax.ppermute(value, "core", [(0, 1), (1, 0)])


def copies_of(value, axes):
    return jnp.broadcast_to(value[None], (lax.axis_size(axes),) + value.shape)


def spread(value, axes):
    return lax.all_to_all(copies_of(value, axes), axes, 0, 0, tiled=True)


def scatter_sum(value, axes):
    size = lax.axis_size(axes)
    blocks = value.reshape((size, value.shape[0] // size) + value.shape[1:])
    received = lax.all_to_all(blocks, axes, 0, 0, tiled=True)
    return jnp.sum(received.astype(F32), axis=0)


def local(query_feats, key_feats, value_feats, out_grad, out_proj, cycle_lo, cycle_hi, lon_half):
    cycles, lon, width = query_feats.shape[1:]
    rows = cycles * lon
    total = cycle_lo.shape[0]
    half_width = width // 2
    q = query_feats.reshape(rows, width)
    k = key_feats.reshape(rows, width)
    v = value_feats.reshape(rows, width)
    grad_flat = out_grad.reshape(rows, width)
    core = lax.axis_index("core")
    mine, others = core * half_width, (1 - core) * half_width

    parts = [
        jnp.stack([k[:, n * PAIR : (n + m) * PAIR], v[:, n * PAIR : (n + m) * PAIR]])
        for n, m in part_pairs(width)
    ]
    below = [lat_shift(part, 1) for part in parts]
    above = [lat_shift(part, -1) for part in parts]
    proj = lax.dynamic_slice_in_dim(out_proj, mine, half_width, axis=1)
    proj = spread(proj, ZY).reshape(-1, half_width)
    proj = copies_of(proj, "x")
    proj, early_q = lax.optimization_barrier((proj, q))
    proj = lax.all_to_all(proj, "x", 0, 0, tiled=True).reshape(-1, half_width)

    latitude = (np.arange(total, dtype=np.float32) + np.float32(0.5)) * np.float32(math.pi / total)
    logw = jnp.asarray(np.log(np.sin(latitude)).astype(np.float32))
    first = (lax.axis_index(LAT) * cycles).astype(jnp.int32).reshape(1)
    band = (first, cycle_lo, cycle_hi, lon_half, logw)
    attended, probs = [], []
    for n in range(HALVES):
        out, prob = forward(n, band, early_q, k, v, below[n], above[n], lon, attended)
        attended = [out]
        probs.append(prob)
    attended = attended[0]

    grad_mine = lax.dynamic_slice_in_dim(grad_flat, mine, half_width, axis=1)
    grad_other = lax.dynamic_slice_in_dim(grad_flat, others, half_width, axis=1)
    sent = dot(attended, grad_other, ((0,), (0,))).astype(BF)
    received = core_swap(sent)
    proj_other = core_swap(proj)
    partial = (dot(attended, grad_mine, ((0,), (0,))) + received.astype(F32)).astype(BF)
    attn_grad = dot(grad_mine, proj, ((1,), (1,))) + dot(grad_other, proj_other, ((1,), (1,)))
    attn_grad = attn_grad.astype(BF)
    whole, edges = [], []
    for n in range(HALVES):
        *whole, low, high = backward(
            n, q, attn_grad, attended, probs[n], k, v, below[n], above[n], lon, whole
        )
        edges.append((low, high))
    query_grad, key_grad, value_grad = whole

    partial = scatter_sum(partial, "x").astype(BF)
    arrived = [(lat_shift(edges[0][1], 1), lat_shift(edges[0][0], -1))]
    partial = scatter_sum(partial, ZY).astype(BF)
    partial, arrived[0] = lax.optimization_barrier((partial, arrived[0]))
    arrived.append((lat_shift(edges[1][1], 1), lat_shift(edges[1][0], -1)))
    samples = lax.axis_size(DP)
    gathered = spread(partial, DP).reshape((samples // 2, 2) + partial.shape)
    summed = jnp.sum(gathered.astype(F32), axis=0)
    scaling = 1.0 / math.sqrt(samples * total * lon)
    proj_grad = jnp.concatenate([summed[0], summed[1]], axis=1) * scaling

    for n, (from_below, from_above) in enumerate(arrived):
        key_grad, value_grad = add_arrived(n, key_grad, value_grad, from_below, from_above)
    shape = query_feats.shape
    return (
        query_grad.reshape(shape),
        key_grad.reshape(shape),
        value_grad.reshape(shape),
        proj_grad,
    )


def solution(mesh):
    parts = Mesh(mesh.devices.reshape(4, 2, 4, 2, 8), DP + LAT)
    placed = P(DP, LAT, None, None)
    return jax.shard_map(
        local,
        mesh=parts,
        in_specs=(placed, placed, placed, placed, P(LAT, None), P(), P(), P()),
        out_specs=(placed, placed, placed, P(LAT, None)),
        check_vma=False,
    )
```

```python
import math

import jax
import jax.numpy as jnp
import numpy as np
from jax import lax
from jax.experimental import pallas as pl
from jax.experimental.pallas import tpu as pltpu
from jax.sharding import Mesh
from jax.sharding import PartitionSpec as P

HEADS = 16
HEAD_DIM = 64
REACH = 2
PAIR = 2 * HEAD_DIM
PPS = 2
HALVES = 2
SCALE = 1.0 / math.sqrt(HEAD_DIM)
SPAN = 2 * REACH + 1
DP = ("zh", "core")
ZY = ("zl", "y")
LAT = ("x", "zl", "y")
BF = jnp.bfloat16
F32 = jnp.float32
VMEM_LIMIT = 32 * 1024 * 1024
LARGE = pl.CostEstimate(flops=2*10**10, bytes_accessed=4*10**7, transcendentals=0)
SMALL = pl.CostEstimate(flops=10**6, bytes_accessed=10**5, transcendentals=0)


def dot(a, b, dims):
    return lax.dot_general(a, b, (dims, ((), ())), preferred_element_type=F32)


def fill_bias(first, lo_ref, hi_ref, half_ref, logw_ref, bias_ref):
    cycles, _, lon = bias_ref.shape
    total = lo_ref.shape[0]
    key_lon = lax.broadcasted_iota(jnp.int32, (lon, lon), 0)
    query_lon = lax.broadcasted_iota(jnp.int32, (lon, lon), 1)
    gap = jnp.abs(key_lon - query_lon)
    dist = jnp.minimum(gap, lon - gap)
    for i in range(cycles):
        cycle = first + i
        lon_ok = dist <= half_ref[cycle]
        for c in range(SPAN):
            key_cycle = cycle - REACH + c
            ok = (key_cycle >= lo_ref[cycle]) & (key_cycle <= hi_ref[cycle])
            weight = logw_ref[jnp.clip(key_cycle, 0, total - 1)]
            value = jnp.where(ok, weight, -jnp.inf)
            bias_ref[i, c * lon : (c + 1) * lon, :] = jnp.where(lon_ok, value, -jnp.inf)


def head_masks(scale):
    lane = lax.broadcasted_iota(jnp.int32, (1, PAIR), 1)
    first = jnp.where(lane < HEAD_DIM, scale, 0.0).astype(F32)
    return first, scale - first


def both_heads(rows, scale):
    first, second = head_masks(scale)
    wide = rows.astype(F32)
    return jnp.concatenate([(wide * first).astype(BF), (wide * second).astype(BF)], axis=0)


def own_columns(both, lon):
    return jnp.concatenate([both[:HEAD_DIM, :lon], both[HEAD_DIM:, lon:]], axis=0).T


def forward_kernel(
    first_ref, lo_ref, hi_ref, half_ref, logw_ref,
    q_ref, kp_ref, ko_ref, kn_ref, vp_ref, vo_ref, vn_ref, *refs,
):
    out_ref, prob_ref, bias_ref = refs[-3:]
    cycles, _, lon = bias_ref.shape

    @pl.when(pl.program_id(0) == 0)
    def _():
        fill_bias(first_ref[0], lo_ref, hi_ref, half_ref, logw_ref, bias_ref)

    units = [(pair, i) for pair in range(PPS) for i in range(cycles)]
    keys, values_t = [], []
    for pair in range(PPS):
        c = slice(pair * PAIR, (pair + 1) * PAIR)
        keys.append(jnp.concatenate([kp_ref[0, :, c], ko_ref[:, c], kn_ref[0, :, c]], axis=0))
        values_t.append(jnp.concatenate([vp_ref[0, :, c], vo_ref[:, c], vn_ref[0, :, c]], axis=0).T)

    def scores_of(unit):
        pair, i = unit
        c = slice(pair * PAIR, (pair + 1) * PAIR)
        queries = both_heads(q_ref[i * lon : (i + 1) * lon, c], SCALE)
        bias = bias_ref.at[i]
        chunks = []
        for n in range(SPAN):
            part = dot(keys[pair][(i + n) * lon : (i + n + 1) * lon], queries, ((1,), (1,)))
            b = bias[n * lon : (n + 1) * lon, :]
            chunks.append(part + jnp.concatenate([b, b], axis=1))
        return chunks

    def finish(unit, chunks):
        pair, i = unit
        c = slice(pair * PAIR, (pair + 1) * PAIR)
        peak = chunks[0]
        for n in chunks[1:]:
            peak = jnp.maximum(peak, n)
        peak = jnp.max(peak, axis=0, keepdims=True)
        chunks = [jnp.exp(n - peak) for n in chunks]
        total = chunks[0]
        for n in chunks[1:]:
            total = total + n
        inverse = 1.0 / jnp.sum(total, axis=0, keepdims=True)
        probs = jnp.concatenate([(n * inverse).astype(BF) for n in chunks], axis=0)
        prob_ref[pair, i] = probs
        window = slice(i * lon, (i + SPAN) * lon)
        attended = dot(values_t[pair][:, window], probs, ((1,), (0,)))
        out_ref[i * lon : (i + 1) * lon, c] = own_columns(attended, lon).astype(BF)

    held = scores_of(units[0])
    for n, unit in enumerate(units):
        later = scores_of(units[n + 1]) if n + 1 < len(units) else None
        finish(unit, held)
        held = later


def backward_kernel(
    q_ref, g_ref, o_ref, prob_ref, kp_ref, ko_ref, kn_ref, vp_ref, vo_ref, vn_ref, *refs,
):
    dq_ref, own_key_ref, own_value_ref, low_ref, high_ref = refs[-5:]
    cycles = prob_ref.shape[1]
    lon = prob_ref.shape[2] // SPAN
    units = [(pair, i) for pair in range(PPS) for i in range(cycles)]
    keys_t, values = [], []
    for pair in range(PPS):
        c = slice(pair * PAIR, (pair + 1) * PAIR)
        keys_t.append(jnp.concatenate([kp_ref[0, :, c], ko_ref[:, c], kn_ref[0, :, c]], axis=0).T)
        values.append(jnp.concatenate([vp_ref[0, :, c], vo_ref[:, c], vn_ref[0, :, c]], axis=0))

    def begin(unit):
        pair, i = unit
        c = slice(pair * PAIR, (pair + 1) * PAIR)
        rows = slice(i * lon, (i + 1) * lon)
        grads = both_heads(g_ref[rows, c], 1.0)
        prob_grad = dot(values[pair][i * lon : (i + SPAN) * lon], grads, ((1,), (1,)))
        product = (g_ref[rows, c].astype(F32) * o_ref[rows, c].astype(F32)).T
        row_dot = jnp.concatenate(
            [
                jnp.sum(product[:HEAD_DIM], axis=0, keepdims=True),
                jnp.sum(product[HEAD_DIM:], axis=0, keepdims=True),
            ],
            axis=1,
        )
        return grads, prob_grad, row_dot

    def finish(unit, held):
        pair, i = unit
        grads, prob_grad, row_dot = held
        c = slice(pair * PAIR, (pair + 1) * PAIR)
        rows = slice(i * lon, (i + 1) * lon)
        window = slice(i * lon, (i + SPAN) * lon)
        probs = prob_ref[pair, i]
        value_part = dot(probs, grads, ((1,), (0,)))
        score_grad = (probs.astype(F32) * (prob_grad - row_dot)).astype(BF)
        queries = both_heads(q_ref[rows, c], SCALE)
        key_part = dot(score_grad, queries, ((1,), (0,)))
        query_part = dot(keys_t[pair][:, window], score_grad, ((1,), (0,)))
        dq_ref[rows, c] = (own_columns(query_part, lon) * SCALE).astype(BF)
        return key_part, value_part

    parts = {}
    held = begin(units[0])
    for n, unit in enumerate(units):
        later = begin(units[n + 1]) if n + 1 < len(units) else None
        parts[unit] = finish(unit, held)
        held = later
        if unit[1] == cycles - 1:
            pair = unit[0]
            c = slice(pair * PAIR, (pair + 1) * PAIR)
            for which in range(2):
                near, far = parts[pair, 0][which], parts[pair, 1][which]
                low_ref[which, :lon, c] = near[:lon].astype(BF)
                low_ref[which, lon:, c] = (near[lon : 2 * lon] + far[:lon]).astype(BF)
                own = near[2 * lon : 4 * lon] + far[lon : 3 * lon]
                (own_key_ref, own_value_ref)[which][:, c] = own.astype(BF)
                high_ref[which, :lon, c] = (near[4 * lon :] + far[3 * lon : 4 * lon]).astype(BF)
                high_ref[which, lon:, c] = far[4 * lon :].astype(BF)


def half_specs(rows, steps, half):
    width = PPS * PAIR
    flat = pl.BlockSpec((rows, width), lambda p: (0, p + half * steps))
    key = pl.BlockSpec((1, rows, width), lambda p: (0, 0, p))
    value = pl.BlockSpec((1, rows, width), lambda p: (1, 0, p))
    both = pl.BlockSpec((2, rows, width), lambda p: (0, 0, p))
    return flat, key, value, both


def forward(half, band, q, k, v, below, above, lon, previous):
    rows, width = q.shape
    cycles = rows // lon
    pairs = width // PAIR // HALVES
    steps = pairs // PPS
    smem = pl.BlockSpec(memory_space=pltpu.SMEM)
    flat, key, value, _ = half_specs(rows, steps, half)
    operands = [*band, q, below, k, above, below, v, above]
    specs = [smem] * len(band) + [flat, key, flat, key, value, flat, value]
    return pl.pallas_call(
        forward_kernel,
        grid=(steps,),
        in_specs=specs + [pl.BlockSpec(memory_space=pl.ANY)] * len(previous),
        out_specs=[flat, pl.BlockSpec((PPS, cycles, SPAN * lon, 2 * lon), lambda p: (p, 0, 0, 0))],
        out_shape=[
            jax.ShapeDtypeStruct((rows, width), BF),
            jax.ShapeDtypeStruct((pairs, cycles, SPAN * lon, 2 * lon), BF),
        ],
        input_output_aliases={len(operands) + n: n for n in range(len(previous))},
        scratch_shapes=[pltpu.VMEM((cycles, SPAN * lon, lon), F32)],
        compiler_params=pltpu.CompilerParams(vmem_limit_bytes=VMEM_LIMIT),
        cost_estimate=LARGE,
        name="attention_forward",
    )(*operands, *previous)


def backward(half, q, g, o, probs, k, v, below, above, lon, previous):
    rows, width = q.shape
    cycles = rows // lon
    pairs = width // PAIR // HALVES
    steps = pairs // PPS
    flat, key, value, both = half_specs(rows, steps, half)
    prob = pl.BlockSpec((PPS, cycles, SPAN * lon, 2 * lon), lambda p: (p, 0, 0, 0))
    whole = jax.ShapeDtypeStruct((rows, width), BF)
    edge = jax.ShapeDtypeStruct((2, rows, width // HALVES), BF)
    operands = [q, g, o, probs, below, k, above, below, v, above]
    specs = [flat, flat, flat, prob, key, flat, key, value, flat, value]
    return pl.pallas_call(
        backward_kernel,
        grid=(steps,),
        in_specs=specs + [pl.BlockSpec(memory_space=pl.ANY)] * len(previous),
        out_specs=[flat, flat, flat, both, both],
        out_shape=[whole, whole, whole, edge, edge],
        input_output_aliases={len(operands) + n: n for n in range(len(previous))},
        compiler_params=pltpu.CompilerParams(vmem_limit_bytes=VMEM_LIMIT),
        cost_estimate=SMALL,
        name="attention_backward",
    )(*operands, *previous)


def total_kernel(below_ref, above_ref, own_key_ref, own_value_ref, key_ref, value_ref):
    for which, (own, out) in enumerate(((own_key_ref, key_ref), (own_value_ref, value_ref))):
        arrived = below_ref[which].astype(F32) + above_ref[which].astype(F32)
        out[...] = (own[...].astype(F32) + arrived).astype(BF)


def add_arrived(half, own_key, own_value, from_below, from_above):
    rows, width = own_key.shape
    steps = width // HALVES // (PPS * PAIR)
    flat, _, _, both = half_specs(rows, steps, half)
    whole = jax.ShapeDtypeStruct((rows, width), BF)
    return pl.pallas_call(
        total_kernel,
        grid=(steps,),
        in_specs=[both, both, flat, flat],
        out_specs=[flat, flat],
        out_shape=[whole, whole],
        input_output_aliases={2: 0, 3: 1},
        cost_estimate=SMALL,
        name="add_arrived",
    )(from_below, from_above, own_key, own_value)


def lat_shift(value, by):
    size = lax.axis_size(LAT)
    pairs = [(i, i + by) for i in range(size) if 0 <= i + by < size]
    return lax.ppermute(value, LAT, pairs)


def core_swap(value):
    return lax.ppermute(value, "core", [(0, 1), (1, 0)])


def copies_of(value, axes):
    return jnp.broadcast_to(value[None], (lax.axis_size(axes),) + value.shape)


def spread(value, axes):
    return lax.all_to_all(copies_of(value, axes), axes, 0, 0, tiled=True)


def scatter_sum(value, axes):
    size = lax.axis_size(axes)
    blocks = value.reshape((size, value.shape[0] // size) + value.shape[1:])
    received = lax.all_to_all(blocks, axes, 0, 0, tiled=True)
    return jnp.sum(received.astype(F32), axis=0)


def local(query_feats, key_feats, value_feats, out_grad, out_proj, cycle_lo, cycle_hi, lon_half):
    cycles, lon, width = query_feats.shape[1:]
    rows = cycles * lon
    total = cycle_lo.shape[0]
    half_width = width // 2
    q = query_feats.reshape(rows, width)
    k = key_feats.reshape(rows, width)
    v = value_feats.reshape(rows, width)
    grad_flat = out_grad.reshape(rows, width)
    core = lax.axis_index("core")
    mine, others = core * half_width, (1 - core) * half_width

    parts = [
        jnp.stack([k[:, n : n + width // HALVES], v[:, n : n + width // HALVES]])
        for n in range(0, width, width // HALVES)
    ]
    below = [lat_shift(part, 1) for part in parts]
    above = [lat_shift(part, -1) for part in parts]
    proj = lax.dynamic_slice_in_dim(out_proj, mine, half_width, axis=1)
    proj = spread(proj, ZY).reshape(-1, half_width)
    proj = copies_of(proj, "x")
    proj, early_q = lax.optimization_barrier((proj, q))
    proj = lax.all_to_all(proj, "x", 0, 0, tiled=True).reshape(-1, half_width)

    latitude = (np.arange(total, dtype=np.float32) + np.float32(0.5)) * np.float32(math.pi / total)
    logw = jnp.asarray(np.log(np.sin(latitude)).astype(np.float32))
    first = (lax.axis_index(LAT) * cycles).astype(jnp.int32).reshape(1)
    band = (first, cycle_lo, cycle_hi, lon_half, logw)
    attended, probs = [], []
    for n in range(HALVES):
        out, prob = forward(n, band, early_q, k, v, below[n], above[n], lon, attended)
        attended = [out]
        probs.append(prob)
    attended = attended[0]

    grad_mine = lax.dynamic_slice_in_dim(grad_flat, mine, half_width, axis=1)
    grad_other = lax.dynamic_slice_in_dim(grad_flat, others, half_width, axis=1)
    sent = dot(attended, grad_other, ((0,), (0,))).astype(BF)
    received = core_swap(sent)
    proj_other = core_swap(proj)
    partial = (dot(attended, grad_mine, ((0,), (0,))) + received.astype(F32)).astype(BF)
    attn_grad = dot(grad_mine, proj, ((1,), (1,))) + dot(grad_other, proj_other, ((1,), (1,)))
    attn_grad = attn_grad.astype(BF)
    whole, edges = [], []
    for n in range(HALVES):
        *whole, low, high = backward(
            n, q, attn_grad, attended, probs[n], k, v, below[n], above[n], lon, whole
        )
        edges.append((low, high))
    query_grad, key_grad, value_grad = whole

    partial = scatter_sum(partial, "x").astype(BF)
    arrived = [(lat_shift(edges[0][1], 1), lat_shift(edges[0][0], -1))]
    partial = scatter_sum(partial, ZY).astype(BF)
    partial, arrived[0] = lax.optimization_barrier((partial, arrived[0]))
    arrived.append((lat_shift(edges[1][1], 1), lat_shift(edges[1][0], -1)))
    samples = lax.axis_size(DP)
    gathered = spread(partial, DP).reshape((samples // 2, 2) + partial.shape)
    summed = jnp.sum(gathered.astype(F32), axis=0)
    scaling = 1.0 / math.sqrt(samples * total * lon)
    proj_grad = jnp.concatenate([summed[0], summed[1]], axis=1) * scaling

    for n, (from_below, from_above) in enumerate(arrived):
        key_grad, value_grad = add_arrived(n, key_grad, value_grad, from_below, from_above)
    shape = query_feats.shape
    return (
        query_grad.reshape(shape),
        key_grad.reshape(shape),
        value_grad.reshape(shape),
        proj_grad,
    )


def solution(mesh):
    parts = Mesh(mesh.devices.reshape(4, 2, 4, 2, 8), DP + LAT)
    placed = P(DP, LAT, None, None)
    return jax.shard_map(
        local,
        mesh=parts,
        in_specs=(placed, placed, placed, placed, P(LAT, None), P(), P(), P()),
        out_specs=(placed, placed, placed, P(LAT, None)),
        check_vma=False,
    )
```
